512 devices in a mesh: rep: 4 (over z_hi, core), expert: 128 (over y, z_lo, x).
Axes of the slice: x: 4, y: 4, z: 16 (z_hi: 2, z_lo: 8; z = z_hi * 8 + z_lo), core: 2. Of those that a mesh axis runs over, the one named last changes fastest.
Arguments:
- tokens: bfloat16 [256, 256, 1280], P('expert', 'rep'), may hold values from -128 to 128, as said below
- router: bfloat16 [1280, 64], replicated, may hold values from -1 to 1
- up_proj: bfloat16 [128, 1280, 1280], P('expert', 'rep'), may hold values from -0.15625 to 0.15625
- down_proj: bfloat16 [128, 1280, 1280], P('expert', 'rep'), may hold values from -0.125 to 0.125
- out_grad: bfloat16 [256, 256, 1280], P('expert', 'rep'), may hold values from -6 to 6
Outputs:
- tokens_grad: bfloat16 [256, 256, 1280], P('expert', 'rep')
- router_grad: float32 [1280, 64], replicated
- up_grad: bfloat16 [128, 1280, 1280], P('expert', 'rep')
- down_grad: bfloat16 [128, 1280, 1280], P('expert', 'rep')
The draws below stay inside these ranges and needn't reach their ends.
Inputs may be any that keep to these rules, and one draw needn't show every extreme that they name: `tokens`: token features.
All inputs are finite; a program needn't handle non-finite values.
Results may differ from the reference program's by a relative error of at most 0.017.
Values may be sent and summed in bfloat16 or wider, within the bound.
No kernel may reach another device: no remote copies, remote signals or barrier semaphores. Data moves between devices by JAX's collectives and lax.ppermute only.
A program may use at most 64 MiB of HBM per device.

```python
import math
import jax
import jax.numpy as jnp
from jax import lax

D = 1280
HID = 2560
TOK_IMG = 256
EXPERTS = 64
IMAGES = 256


def router_field(key):
    return jax.random.truncated_normal(key, -4.0, 4.0, (D, EXPERTS), jnp.float32) * (1.0 / math.sqrt(D))


def draw_router(key, part):
    field = router_field(key)
    return field.astype(jnp.bfloat16)


def draw_tokens(key, part):
    key = jax.random.fold_in(key, 3)
    subkeys = jax.random.split(key, 1)
    features = jax.random.truncated_normal(subkeys[0], -6.0, 6.0, (IMAGES, TOK_IMG, D), jnp.float32)
    return features.astype(jnp.bfloat16)


def shard_levels(stream_key, shape, cuts, smallest, top_value):
    level, own = 1.0, jax.random.fold_in(stream_key, 6)
    for axis_at, parts in cuts:
        steps = jnp.exp(jax.random.uniform(jax.random.fold_in(own, axis_at), (parts,), jnp.float32, smallest / len(cuts), top_value / len(cuts)))
        level = level * jnp.repeat(steps, shape[axis_at] // parts).reshape([-1 if axis == axis_at else 1 for axis in range(len(shape))])
    return level


def noise(key, extent, spread, reach, cuts=(), kind=jnp.bfloat16):
    factor_of = shard_levels(key, extent, cuts, -0.22, 0.18) if cuts else 1.0
    result = jax.random.normal(key, extent, jnp.float32) * spread * factor_of
    return jnp.minimum(jnp.maximum(result, -reach), reach).astype(kind)


def setup_inputs(seed: int = 0) -> dict:
    key_of = jax.random.split(jax.random.key(seed), 6)
    tokens = draw_tokens(jax.random.fold_in(key_of[5], 71), 0)
    router = draw_router(jax.random.fold_in(key_of[5], 71), 0)
    up_proj = noise(key_of[2], (2 * EXPERTS, HID // 2, D), D ** -0.5, 0.15625, ((0, 128), (1, 4)))
    down_proj = noise(key_of[3], (2 * EXPERTS, HID // 2, D), HID ** -0.5, 0.125, ((0, 128), (1, 4)))
    out_grad = noise(key_of[4], (IMAGES, TOK_IMG, D), 1.0, 6.0, ((0, 128), (1, 4)))
    return {"tokens": tokens, "router": router, "up_proj": up_proj, "down_proj": down_proj, "out_grad": out_grad}


def gelu_exact(values):
    return jax.nn.gelu(values, approximate=False)

def expert_step(inputs):
    slot_rows, grad_rows, w_up, w_down = inputs
    pre_act = jnp.dot(slot_rows, w_up.T, preferred_element_type=jnp.float32)
    hidden = gelu_exact(pre_act).astype(jnp.bfloat16)
    slot_out = jnp.dot(hidden, w_down, preferred_element_type=jnp.float32).astype(jnp.bfloat16)
    hid_grad = jnp.dot(grad_rows, w_down.T, preferred_element_type=jnp.float32)
    unused, gelu_pull = jax.vjp(gelu_exact, pre_act)
    pre_grad = gelu_pull(hid_grad)[0].astype(jnp.bfloat16)
    up_part = jnp.dot(pre_grad.T, slot_rows, preferred_element_type=jnp.float32).astype(jnp.bfloat16)
    down_part = jnp.dot(hidden.T, grad_rows, preferred_element_type=jnp.float32).astype(jnp.bfloat16)
    in_grad = jnp.dot(pre_grad, w_up, preferred_element_type=jnp.float32).astype(jnp.bfloat16)
    return (slot_out, in_grad, up_part, down_part)

def reference(tokens, router, up_proj, down_proj, out_grad):
    tok_wide = tokens.astype(jnp.float32)
    grad_wide = out_grad.astype(jnp.float32)
    router_wide = router.astype(jnp.float32)
    logits = jnp.einsum('btd,ds->bts', tok_wide, router_wide)
    dispatch = jax.nn.softmax(logits, axis=1)
    combine = jax.nn.softmax(logits, axis=2)
    dispatch_w = dispatch.astype(jnp.bfloat16)
    combine_w = combine.astype(jnp.bfloat16)
    slot_in = jnp.einsum('bts,btd->bsd', dispatch_w.astype(jnp.float32), tok_wide).astype(jnp.bfloat16)
    slot_grad = jnp.einsum('bts,btd->bsd', combine_w.astype(jnp.float32), grad_wide).astype(jnp.bfloat16)
    w_up = up_proj.reshape(EXPERTS, HID, D)
    w_down = down_proj.reshape(EXPERTS, HID, D)
    slot_out, slot_in_grad, up_parts, down_parts = lax.map(expert_step, (slot_in.transpose(1, 0, 2), slot_grad.transpose(1, 0, 2), w_up, w_down))
    slot_out = slot_out.transpose(1, 0, 2).astype(jnp.float32)
    slot_in_grad = slot_in_grad.transpose(1, 0, 2).astype(jnp.float32)
    up_grad = up_parts.reshape(2 * EXPERTS, HID // 2, D)
    down_grad = down_parts.reshape(2 * EXPERTS, HID // 2, D)
    cgrad = jnp.einsum('btd,bsd->bts', grad_wide, slot_out)
    dgrad = jnp.einsum('btd,bsd->bts', tok_wide, slot_in_grad)
    comb_part = combine * (cgrad - lax.optimization_barrier(jnp.sum(combine * cgrad, axis=2, keepdims=True)))
    disp_part = dispatch * (dgrad - lax.optimization_barrier(jnp.sum(dispatch * dgrad, axis=1, keepdims=True)))
    logit_grad = (comb_part + disp_part).astype(jnp.bfloat16).astype(jnp.float32)
    tokens_grad = (jnp.einsum('bts,bsd->btd', dispatch_w.astype(jnp.float32), slot_in_grad) + jnp.einsum('bts,ds->btd', logit_grad, router_wide)).astype(jnp.bfloat16)
    router_grad = jnp.einsum('btd,bts->ds', tok_wide, logit_grad)
    return (tokens_grad, router_grad, up_grad, down_grad)
```

```python
import functools
import jax
import jax.numpy as jnp
from jax import lax
from jax.experimental import pallas as pl
from jax.experimental.pallas import tpu as pltpu
from jax.sharding import Mesh, PartitionSpec as P

D = 1280
LANES = 128
WIDE = D + LANES
SLOTS = 64
Y, ZL, XH = 4, 8, 2
PLANE = ("y", "xh", "xl")
COLUMN = ("zh", "zl")
EVERY_GROUP = ("y", "zl", "xh", "xl")
bf16, f32 = jnp.bfloat16, jnp.float32
NT = (((1,), (1,)), ((), ()))
TN = (((0,), (0,)), ((), ()))
SMEM = pl.BlockSpec(memory_space=pltpu.SMEM)
VMEM = pl.BlockSpec(memory_space=pltpu.VMEM)


def call(kernel, outs, *operands, flops=0):
    bytes_accessed = sum(a.size * a.dtype.itemsize for a in list(operands) + list(outs))
    return pl.pallas_call(
        kernel,
        out_shape=outs,
        in_specs=[SMEM] + [VMEM] * (len(operands) - 1),
        out_specs=[VMEM] * len(outs),
        compiler_params=pltpu.CompilerParams(vmem_limit_bytes=48 * 1024 * 1024),
        cost_estimate=pl.CostEstimate(flops=flops, bytes_accessed=bytes_accessed, transcendentals=0),
    )(*operands)


def shaped(shape, dtype):
    return jax.ShapeDtypeStruct(shape, dtype)


def pieces(value):
    first = value.astype(bf16).astype(f32)
    second = (value - first).astype(bf16).astype(f32)
    third = (value - first - second).astype(bf16).astype(f32)
    return [first, second, third]


def lanes_of(columns):
    rows = columns[0].shape[0]
    lane = lax.broadcasted_iota(jnp.int32, (rows, LANES), 1)
    packed = jnp.zeros((rows, LANES), f32)
    for k, column in enumerate(columns):
        packed = jnp.where(lane == k, column, packed)
    return packed


def three(stats, first):
    return stats[:, first : first + 1] + stats[:, first + 1 : first + 2] + stats[:, first + 2 : first + 3]


def combine_of(logits):
    raised = jnp.exp(logits - jnp.max(logits, axis=0, keepdims=True))
    return raised / jnp.sum(raised, axis=0, keepdims=True)


def slots_kernel(core, router_t, tok_a, tok_b, grad_a, grad_b, out):
    on_first = core[0] == 0
    rows = []
    for image in range(2):
        tok = jnp.concatenate([tok_a[image], tok_b[image]], axis=0)
        grad = jnp.concatenate([grad_a[image], grad_b[image]], axis=0)
        logits = lax.dot_general(router_t[...], tok, NT, preferred_element_type=f32)
        top = jnp.max(logits, axis=1, keepdims=True)
        raised = jnp.exp(logits - top)
        total = jnp.sum(raised, axis=1, keepdims=True)
        weights = jnp.where(on_first, raised / total, combine_of(logits)).astype(bf16)
        data = jnp.where(on_first, tok, grad)
        part = jnp.dot(weights, data, preferred_element_type=f32)
        rows.append((part, lanes_of(pieces(top) + pieces(total))))
    for zl in range(ZL):
        at = slice(zl * 8, zl * 8 + 8)
        for zh in range(2):
            place = zh * ZL + zl
            out[place, :, :D] = jnp.concatenate([rows[0][0][at], rows[1][0][at]], axis=0).astype(bf16)
            out[place, :, D:] = jnp.concatenate([rows[0][1][at], rows[1][1][at]], axis=0).astype(bf16)


def middle_kernel(core, got, out, kept, stats_out):
    on_first = core[0] == 0
    stats = [got[h * ZL : (h + 1) * ZL, :, D:].reshape(LANES, LANES).astype(f32) for h in range(2)]
    tops = [three(s, 0) for s in stats]
    totals = [three(s, 3) for s in stats]
    top = jnp.maximum(tops[0], tops[1])
    parts = [totals[h] * jnp.exp(tops[h] - top) for h in range(2)]
    total = parts[0] + parts[1]
    shares = [jnp.where(on_first, part / total, 1.0) for part in parts]
    halves = [got[h * ZL : (h + 1) * ZL, :, :D].reshape(LANES, D).astype(f32) for h in range(2)]
    summed = halves[0] * shares[0] + halves[1] * shares[1]
    kept[...] = summed
    stats_out[...] = lanes_of([top, total])
    row = lax.broadcasted_iota(jnp.int32, (LANES, LANES), 0)
    col = lax.broadcasted_iota(jnp.int32, (LANES, LANES), 1)
    source = ((row & 15) >> 1) * 16 + (row & 1) * 8 + (row >> 4)
    pick = jnp.where(col == source, 1.0, 0.0).astype(bf16)
    sorted_rows = jnp.dot(pick, summed.astype(bf16), preferred_element_type=f32).astype(bf16)
    for yx in range(Y * XH):
        for xl in range(2):
            out[2 * yx + xl] = sorted_rows[yx * 16 : yx * 16 + 16]


def expert_kernel(core, mine, other, w_up, w_down, up_grad, down_grad, keep, send):
    on_first = core[0] == 0
    slot_in = jnp.where(on_first, mine[...], other[...])
    slot_grad = jnp.where(on_first, other[...], mine[...])
    pre_act = lax.dot_general(slot_in, w_up[...], NT, preferred_element_type=f32)
    hid_grad = lax.dot_general(slot_grad, w_down[...], NT, preferred_element_type=f32)
    cdf = 0.5 * (1.0 + lax.erf(pre_act * 0.7071067811865476))
    density = jnp.exp(pre_act * pre_act * -0.5) * 0.3989422804014327
    hidden = (pre_act * cdf).astype(bf16)
    pre_grad = (hid_grad * (cdf + pre_act * density)).astype(bf16)
    slot_out = jnp.dot(hidden, w_down[...], preferred_element_type=f32)
    in_grad = jnp.dot(pre_grad, w_up[...], preferred_element_type=f32)
    keep[...] = jnp.where(on_first, in_grad, slot_out)
    send[...] = jnp.where(on_first, slot_out, in_grad).astype(bf16)
    up_grad[0] = lax.dot_general(pre_grad, slot_in, TN, preferred_element_type=f32).astype(bf16)
    down_grad[0] = lax.dot_general(hidden, slot_grad, TN, preferred_element_type=f32).astype(bf16)


def return_kernel(core, got, kept, stats, out):
    row = lax.broadcasted_iota(jnp.int32, (LANES, 2 * LANES), 0)
    col = lax.broadcasted_iota(jnp.int32, (LANES, 2 * LANES), 1)
    source = (row & 7) * 32 + (row >> 4) * 2 + ((row >> 3) & 1)
    pick = jnp.where((col & ~16) == source, 1.0, 0.0).astype(bf16)
    summed = jnp.dot(pick, got[...], preferred_element_type=f32).astype(bf16)
    share = jnp.sum(kept[...] * summed.astype(f32), axis=1, keepdims=True)
    top, total = stats[:, 0:1], stats[:, 1:2]
    extra = lanes_of(pieces(share) + pieces(top) + pieces(total)).astype(bf16)
    for zl in range(ZL):
        at = slice(zl * 16, zl * 16 + 16)
        for zh in range(2):
            out[zh * ZL + zl, :, :D] = summed[at]
            out[zh * ZL + zl, :, D:] = extra[at]


def tokens_kernel(core, router_t, tok_a, tok_b, grad_a, grad_b, mine, other, tokens_grad, router_grad):
    on_first = core[0] == 0
    back = [jnp.where(on_first, mine[h * ZL : (h + 1) * ZL], other[h * ZL : (h + 1) * ZL]).astype(f32) for h in range(2)]
    outs = [jnp.where(on_first, other[h * ZL : (h + 1) * ZL], mine[h * ZL : (h + 1) * ZL]).astype(f32) for h in range(2)]
    back_sum = back[0] + back[1]
    outs_sum = outs[0] + outs[1]
    router_sum = jnp.zeros((SLOTS, D), f32)
    for image in range(2):
        at = slice(image * 8, image * 8 + 8)
        slot_in_grad = back_sum[:, at, :D].reshape(SLOTS, D).astype(bf16)
        slot_out = outs_sum[:, at, :D].reshape(SLOTS, D).astype(bf16)
        weighted = three(back_sum[:, at, D:].reshape(SLOTS, LANES), 0)
        stats = back[0][:, at, D:].reshape(SLOTS, LANES)
        top, total = three(stats, 3), three(stats, 6)
        tok = jnp.concatenate([tok_a[image], tok_b[image]], axis=0)
        grad = jnp.concatenate([grad_a[image], grad_b[image]], axis=0)
        logits = lax.dot_general(router_t[...], tok, NT, preferred_element_type=f32)
        dispatch = jnp.exp(logits - top) / total
        combine = combine_of(logits)
        cgrad = lax.dot_general(slot_out, grad, NT, preferred_element_type=f32)
        dgrad = lax.dot_general(slot_in_grad, tok, NT, preferred_element_type=f32)
        comb_part = combine * (cgrad - jnp.sum(combine * cgrad, axis=0, keepdims=True))
        disp_part = dispatch * (dgrad - weighted)
        logit_grad = comb_part + disp_part
        router_sum += jnp.dot(logit_grad.astype(bf16), tok, preferred_element_type=f32)
        left = jnp.concatenate([dispatch[:, :64], logit_grad[:, :64]], axis=0).astype(bf16)
        right = jnp.concatenate([slot_in_grad, router_t[...]], axis=0)
        tokens_grad[image] = lax.dot_general(left, right, TN, preferred_element_type=f32).astype(bf16)
    router_grad[...] = router_sum.astype(bf16)


def swap(value):
    return lax.ppermute(value, "core", [(0, 1), (1, 0)])


def exchange(value, axes):
    return lax.all_to_all(value, axes, split_axis=0, concat_axis=0, tiled=True)


def on_device(tokens, router, up_proj, down_proj, out_grad):
    core = lax.axis_index("core").astype(jnp.int32).reshape(1)
    router_t = router.T.reshape(Y, ZL, XH, D).transpose(1, 0, 2, 3).reshape(SLOTS, D)
    tok_b, grad_b = swap(tokens), swap(out_grad)
    (slots,) = call(
        slots_kernel, [shaped((16, 16, WIDE), bf16)], core, router_t, tokens, tok_b, out_grad, grad_b
    )
    got = exchange(slots, COLUMN)
    by_expert, kept, stats = call(
        middle_kernel,
        [shaped((16, 16, D), bf16), shaped((LANES, D), f32), shaped((LANES, LANES), f32)],
        core, got,
    )
    mine = exchange(by_expert, PLANE).reshape(256, D)
    other = swap(mine)
    up_grad, down_grad, keep, send = call(
        expert_kernel,
        [shaped((1, 320, D), bf16), shaped((1, 320, D), bf16), shaped((256, D), f32), shaped((256, D), bf16)],
        core, mine, other, up_proj[0], down_proj[0],
    )
    summed = (keep + swap(send).astype(f32)).astype(bf16).reshape(16, 16, D)
    back = exchange(summed, PLANE).reshape(256, D)
    (by_owner,) = call(return_kernel, [shaped((16, 16, WIDE), bf16)], core, back, kept, stats)
    mine = exchange(by_owner, COLUMN)
    other = swap(mine)
    tokens_grad, router_part = call(
        tokens_kernel,
        [shaped((2, 64, D), bf16), shaped((SLOTS, D), bf16)],
        core, router_t, tokens, tok_b, out_grad, grad_b, mine, other,
    )
    part = exchange(router_part.reshape(16, 4, D), PLANE).astype(f32).sum(axis=0).astype(bf16)
    whole = exchange(jnp.broadcast_to(part, (16, 4, D)), COLUMN).astype(f32).sum(axis=0).astype(bf16)
    full = exchange(jnp.broadcast_to(whole, (16, 4, D)), PLANE).reshape(ZL, Y, XH, D)
    router_grad = full.transpose(1, 0, 2, 3).reshape(SLOTS, D).T.astype(f32)
    return tokens_grad, router_grad, up_grad, down_grad


def solution(mesh):
    fine = Mesh(mesh.devices.reshape(2, 2, Y, ZL, XH, 2), ("zh", "core", "y", "zl", "xh", "xl"))
    rows = P(EVERY_GROUP, ("zh", "core"), None)
    return jax.shard_map(
        on_device,
        mesh=fine,
        in_specs=(rows, P(), rows, rows, rows),
        out_specs=(rows, P(), rows, rows),
        check_vma=False,
    )
```

```python
import jax
import jax.numpy as jnp
from jax import lax
from jax.experimental import pallas as pl
from jax.experimental.pallas import tpu as pltpu
from jax.sharding import Mesh, PartitionSpec as P

D = 1280
LANES = 128
WIDE = D + LANES
SLOTS = 64
Y, ZL, XH = 4, 8, 2
PLANE = ("y", "xh", "xl")
PLANE_CORES = ("core", "y", "xh", "xl")
COLUMN = ("zh", "zl")
EVERY_GROUP = ("y", "zl", "xh", "xl")
bf16, f32 = jnp.bfloat16, jnp.float32
NT = (((1,), (1,)), ((), ()))
TN = (((0,), (0,)), ((), ()))
SMEM = pl.BlockSpec(memory_space=pltpu.SMEM)
VMEM = pl.BlockSpec(memory_space=pltpu.VMEM)
ANY = pl.BlockSpec(memory_space=pl.ANY)


def call(kernel, outs, *operands, after=()):
    body = kernel
    if after:
        first, last = len(operands), len(operands) + len(after)
        body = lambda *refs: kernel(*refs[:first], *refs[last:])
    bytes_accessed = sum(a.size * a.dtype.itemsize for a in list(operands) + list(outs))
    return pl.pallas_call(
        body,
        out_shape=outs,
        in_specs=[SMEM] + [VMEM] * (len(operands) - 1) + [ANY] * len(after),
        out_specs=[VMEM] * len(outs),
        compiler_params=pltpu.CompilerParams(vmem_limit_bytes=48 * 1024 * 1024),
        cost_estimate=pl.CostEstimate(flops=0, bytes_accessed=bytes_accessed, transcendentals=0),
    )(*operands, *after)


def shaped(shape, dtype):
    return jax.ShapeDtypeStruct(shape, dtype)


def pieces(value):
    first = value.astype(bf16).astype(f32)
    second = (value - first).astype(bf16).astype(f32)
    third = (value - first - second).astype(bf16).astype(f32)
    return [first, second, third]


def lanes_of(columns):
    rows = columns[0].shape[0]
    lane = lax.broadcasted_iota(jnp.int32, (rows, LANES), 1)
    packed = jnp.zeros((rows, LANES), f32)
    for k, column in enumerate(columns):
        packed = jnp.where(lane == k, column, packed)
    return packed


def three(stats, first):
    return stats[:, first : first + 1] + stats[:, first + 1 : first + 2] + stats[:, first + 2 : first + 3]


def combine_of(logits):
    raised = jnp.exp(logits - jnp.max(logits, axis=0, keepdims=True))
    return raised / jnp.sum(raised, axis=0, keepdims=True)


def slots_kernel(where_am_i, router_t, tok_a, tok_b, grad_a, grad_b, keep, send):
    on_first, zh = where_am_i[0] == 0, where_am_i[1]
    for image, out in ((1 - zh, send), (zh, keep)):
        tok = jnp.concatenate([tok_a[image], tok_b[image]], axis=0)
        grad = jnp.concatenate([grad_a[image], grad_b[image]], axis=0)
        logits = lax.dot_general(router_t[...], tok, NT, preferred_element_type=f32)
        top = jnp.max(logits, axis=1, keepdims=True)
        raised = jnp.exp(logits - top)
        total = jnp.sum(raised, axis=1, keepdims=True)
        weights = jnp.where(on_first, raised / total, combine_of(logits)).astype(bf16)
        data = jnp.where(on_first, tok, grad)
        out[:, :D] = jnp.dot(weights, data, preferred_element_type=f32).astype(out.dtype)
        out[:, D:] = lanes_of(pieces(top) + pieces(total)).astype(out.dtype)


def join_kernel(where_am_i, keep, got, out):
    on_first = where_am_i[0] == 0
    halves = [keep[...], got[...].astype(f32)]
    tops = [three(h[:, D:], 0) for h in halves]
    totals = [three(h[:, D:], 3) for h in halves]
    top = jnp.maximum(tops[0], tops[1])
    parts = [totals[h] * jnp.exp(tops[h] - top) for h in range(2)]
    total = parts[0] + parts[1]
    shares = [jnp.where(on_first, part / total, 1.0) for part in parts]
    rows = (halves[0][:, :D] * shares[0] + halves[1][:, :D] * shares[1]).astype(bf16)
    out[0] = rows
    out[1] = rows


def middle_kernel(where_am_i, got, tok_a, grad_a, out, tok_out, grad_out):
    zh = where_am_i[1]
    row = lax.broadcasted_iota(jnp.int32, (LANES, LANES), 0)
    col = lax.broadcasted_iota(jnp.int32, (LANES, LANES), 1)
    pick = jnp.where(col == (row & 15) * 8 + (row >> 4), 1.0, 0.0).astype(bf16)
    sorted_rows = jnp.dot(pick, got[...], preferred_element_type=f32).astype(bf16)
    for yx in range(Y * XH):
        for xl in range(2):
            out[2 * yx + xl] = sorted_rows[yx * 16 : yx * 16 + 16]
    tok_out[...] = tok_a[1 - zh]
    grad_out[...] = grad_a[1 - zh]


def expert_kernel(where_am_i, mine, other, w_up, w_down, up_grad, down_grad, keep, send):
    on_first = where_am_i[0] == 0
    slot_in = jnp.where(on_first, mine[...], other[...])
    slot_grad = jnp.where(on_first, other[...], mine[...])
    pre_act = lax.dot_general(slot_in, w_up[...], NT, preferred_element_type=f32)
    hid_grad = lax.dot_general(slot_grad, w_down[...], NT, preferred_element_type=f32)
    cdf = 0.5 * (1.0 + lax.erf(pre_act * 0.7071067811865476))
    density = jnp.exp(pre_act * pre_act * -0.5) * 0.3989422804014327
    hidden = (pre_act * cdf).astype(bf16)
    pre_grad = (hid_grad * (cdf + pre_act * density)).astype(bf16)
    slot_out = jnp.dot(hidden, w_down[...], preferred_element_type=f32)
    in_grad = jnp.dot(pre_grad, w_up[...], preferred_element_type=f32)
    keep[...] = jnp.where(on_first, in_grad, slot_out)
    send[...] = jnp.where(on_first, slot_out, in_grad).astype(bf16)
    up_grad[0] = lax.dot_general(pre_grad, slot_in, TN, preferred_element_type=f32).astype(bf16)
    down_grad[0] = lax.dot_general(hidden, slot_grad, TN, preferred_element_type=f32).astype(bf16)


def return_kernel(where_am_i, got, out):
    row = lax.broadcasted_iota(jnp.int32, (LANES, 2 * LANES), 0)
    col = lax.broadcasted_iota(jnp.int32, (LANES, 2 * LANES), 1)
    pick = jnp.where((col & ~16) == (row & 7) * 32 + (row >> 3), 1.0, 0.0).astype(bf16)
    out[...] = jnp.dot(pick, got[...], preferred_element_type=f32).astype(bf16)


def halves_kernel(where_am_i, got, out):
    out[...] = (got[:SLOTS].astype(f32) + got[SLOTS:].astype(f32)).astype(bf16)


def tokens_kernel(
    where_am_i, router_t, tok_a, tok_b, tok_c, tok_d, grad_a, grad_b, grad_c, grad_d, mine, other,
    own_grad, sent_grad, router_grad,
):
    on_first, zh = where_am_i[0] == 0, where_am_i[1]

    slot_in_grad = jnp.where(on_first, mine[...], other[...])
    slot_out = jnp.where(on_first, other[...], mine[...])
    tok = jnp.concatenate([tok_a[zh], tok_c[...], tok_b[zh], tok_d[...]], axis=0)
    grad = jnp.concatenate([grad_a[zh], grad_c[...], grad_b[zh], grad_d[...]], axis=0)
    logits = lax.dot_general(router_t[...], tok, NT, preferred_element_type=f32)
    raised = jnp.exp(logits - jnp.max(logits, axis=1, keepdims=True))
    dispatch = raised / jnp.sum(raised, axis=1, keepdims=True)
    combine = combine_of(logits)
    cgrad = lax.dot_general(slot_out, grad, NT, preferred_element_type=f32)
    dgrad = lax.dot_general(slot_in_grad, tok, NT, preferred_element_type=f32)
    comb_part = combine * (cgrad - jnp.sum(combine * cgrad, axis=0, keepdims=True))
    disp_part = dispatch * (dgrad - jnp.sum(dispatch * dgrad, axis=1, keepdims=True))
    logit_grad = (comb_part + disp_part)[:, :LANES].astype(bf16)
    router_grad[...] = jnp.dot(logit_grad, tok[:LANES], preferred_element_type=f32).astype(bf16)
    left = jnp.concatenate([dispatch[:, :LANES].astype(bf16), logit_grad], axis=0)
    right = jnp.concatenate([slot_in_grad, router_t[...]], axis=0)
    both = lax.dot_general(left, right, TN, preferred_element_type=f32).astype(bf16)
    own_grad[...] = both[:64]
    sent_grad[...] = both[64:]


def fence_kernel(where_am_i, value, out):
    out[...] = value[...]


def swap(value, axis="core"):
    return lax.ppermute(value, axis, [(0, 1), (1, 0)])


def exchange(value, axes):
    return lax.all_to_all(value, axes, split_axis=0, concat_axis=0, tiled=True)


def on_device(tokens, router, up_proj, down_proj, out_grad):
    zh = lax.axis_index("zh").astype(jnp.int32)
    here = jnp.stack([lax.axis_index("core").astype(jnp.int32), zh])
    router_t = router.T.reshape(Y, ZL, XH, D).transpose(1, 0, 2, 3).reshape(SLOTS, D)
    tok_b, grad_b = swap(tokens), swap(out_grad)
    keep, send = call(
        slots_kernel,
        [shaped((SLOTS, WIDE), f32), shaped((SLOTS, WIDE), bf16)],
        here, router_t, tokens, tok_b, out_grad, grad_b,
    )
    (slots,) = call(join_kernel, [shaped((2, SLOTS, D), bf16)], here, keep, swap(send, "zh"))
    got = exchange(slots.reshape(16, 8, D), COLUMN).reshape(LANES, D)
    by_expert, tok_send, grad_send = call(
        middle_kernel,
        [shaped((16, 16, D), bf16), shaped((64, D), bf16), shaped((64, D), bf16)],
        here, got, tokens, out_grad,
    )
    tok_c, grad_c = swap(tok_send, "zh"), swap(grad_send, "zh")
    tok_d, grad_d = swap(tok_c), swap(grad_c)
    got = exchange(by_expert, PLANE).reshape(256, D)
    (mine,) = call(fence_kernel, [shaped((256, D), bf16)], here, got, after=(tok_c,))
    other = swap(mine)
    up_grad, down_grad, keep, send = call(
        expert_kernel,
        [shaped((1, 320, D), bf16), shaped((1, 320, D), bf16), shaped((256, D), f32), shaped((256, D), bf16)],
        here, mine, other, up_proj[0], down_proj[0],
    )
    summed = (keep + swap(send).astype(f32)).astype(bf16).reshape(16, 16, D)
    back = exchange(summed, PLANE).reshape(256, D)
    (by_owner,) = call(return_kernel, [shaped((LANES, D), bf16)], here, back, after=(tok_d, grad_c))
    got = exchange(by_owner.reshape(16, 8, D), COLUMN).reshape(LANES, D)
    (mine,) = call(halves_kernel, [shaped((SLOTS, D), bf16)], here, got, after=(grad_d,))
    other = swap(mine)
    own_grad, sent_grad, router_part = call(
        tokens_kernel,
        [shaped((64, D), bf16), shaped((64, D), bf16), shaped((SLOTS, D), bf16)],
        here, router_t, tokens, tok_b, tok_c, tok_d, out_grad, grad_b, grad_c, grad_d, mine, other,
    )
    got_grad = swap(sent_grad, "zh")
    tokens_grad = jnp.where(zh == 0, jnp.stack([own_grad, got_grad]), jnp.stack([got_grad, own_grad]))
    part = exchange(router_part.reshape(32, 2, D), PLANE_CORES).astype(f32).sum(axis=0).astype(bf16)
    whole = exchange(jnp.broadcast_to(part, (16, 2, D)), COLUMN).astype(f32).sum(axis=0).astype(bf16)
    full = exchange(jnp.broadcast_to(whole, (32, 2, D)), PLANE_CORES).reshape(ZL, Y, XH, D)
    router_grad = full.transpose(1, 0, 2, 3).reshape(SLOTS, D).T.astype(f32)
    return tokens_grad, router_grad, up_grad, down_grad


def solution(mesh):
    fine = Mesh(mesh.devices.reshape(2, 2, Y, ZL, XH, 2), ("zh", "core", "y", "zl", "xh", "xl"))
    rows = P(EVERY_GROUP, ("zh", "core"), None)
    return jax.shard_map(
        on_device,
        mesh=fine,
        in_specs=(rows, P(), rows, rows, rows),
        out_specs=(rows, P(), rows, rows),
        check_vma=False,
    )
```

```python
import jax
import jax.numpy as jnp
from jax import lax
from jax.experimental import pallas as pl
from jax.experimental.pallas import tpu as pltpu
from jax.sharding import Mesh, PartitionSpec as P

D = 1280
LANES = 128
WIDE = D + LANES
SLOTS = 64
Y, ZL, XH = 4, 8, 2
PLANE = ("y", "xh", "xl")
PLANE_CORES = ("core", "y", "xh", "xl")
COLUMN = ("zh", "zl")
EVERY_GROUP = ("y", "zl", "xh", "xl")
bf16, f32 = jnp.bfloat16, jnp.float32
NT = (((1,), (1,)), ((), ()))
TN = (((0,), (0,)), ((), ()))
SMEM = pl.BlockSpec(memory_space=pltpu.SMEM)
VMEM = pl.BlockSpec(memory_space=pltpu.VMEM)
ANY = pl.BlockSpec(memory_space=pl.ANY)
HBM = pl.BlockSpec(memory_space=pltpu.HBM)


def call(kernel, outs, *operands, after=()):
    body = kernel
    if after:
        first, last = len(operands), len(operands) + len(after)
        body = lambda *refs: kernel(*refs[:first], *refs[last:])
    bytes_accessed = sum(a.size * a.dtype.itemsize for a in list(operands) + list(outs))
    return pl.pallas_call(
        body,
        out_shape=outs,
        in_specs=[SMEM] + [VMEM] * (len(operands) - 1) + [ANY] * len(after),
        out_specs=[VMEM] * len(outs),
        compiler_params=pltpu.CompilerParams(vmem_limit_bytes=20 * 1024 * 1024),
        cost_estimate=pl.CostEstimate(flops=0, bytes_accessed=bytes_accessed, transcendentals=0),
    )(*operands, *after)


def shaped(shape, dtype):
    return jax.ShapeDtypeStruct(shape, dtype)


def pieces(value):
    first = value.astype(bf16).astype(f32)
    second = (value - first).astype(bf16).astype(f32)
    third = (value - first - second).astype(bf16).astype(f32)
    return [first, second, third]


def lanes_of(columns):
    rows = columns[0].shape[0]
    lane = lax.broadcasted_iota(jnp.int32, (rows, LANES), 1)
    packed = jnp.zeros((rows, LANES), f32)
    for k, column in enumerate(columns):
        packed = jnp.where(lane == k, column, packed)
    return packed


def three(stats, first):
    return stats[:, first : first + 1] + stats[:, first + 1 : first + 2] + stats[:, first + 2 : first + 3]


def combine_of(logits):
    raised = jnp.exp(logits - jnp.max(logits, axis=0, keepdims=True))
    return raised / jnp.sum(raised, axis=0, keepdims=True)


def slot_order(transpose=False):
    own = lax.broadcasted_iota(jnp.int32, (SLOTS, SLOTS), 1 if transpose else 0)
    expert = lax.broadcasted_iota(jnp.int32, (SLOTS, SLOTS), 0 if transpose else 1)
    return jnp.where(expert == ((own >> 1) & 3) * 16 + (own >> 3) * 2 + (own & 1), 1.0, 0.0).astype(bf16)


def merged(on_first, halves):
    tops = [three(h[:, D:], 0) for h in halves]
    totals = [three(h[:, D:], 3) for h in halves]
    top = jnp.maximum(tops[0], tops[1])
    parts = [totals[h] * jnp.exp(tops[h] - top) for h in range(2)]
    total = parts[0] + parts[1]
    shares = [jnp.where(on_first, part / total, 1.0) for part in parts]
    return halves[0][:, :D] * shares[0] + halves[1][:, :D] * shares[1], top, total


def slots_kernel(where_am_i, router_rows, tok_a, tok_b, grad_a, grad_b, out, router_t):
    core = where_am_i[0]
    router_t[...] = jnp.dot(slot_order(), router_rows[...], preferred_element_type=f32).astype(bf16)
    tok = jnp.concatenate([tok_a[core], tok_b[core]], axis=0)
    grad = jnp.concatenate([grad_a[core], grad_b[core]], axis=0)
    logits = lax.dot_general(router_t[...], tok, NT, preferred_element_type=f32)
    top = jnp.max(logits, axis=1, keepdims=True)
    raised = jnp.exp(logits - top)
    total = jnp.sum(raised, axis=1, keepdims=True)
    stats = lanes_of(pieces(top) + pieces(total))
    part_in = jnp.dot((raised / total).astype(bf16), tok, preferred_element_type=f32)
    part_grad = jnp.dot(combine_of(logits).astype(bf16), grad, preferred_element_type=f32)
    for zl in range(ZL):
        at = slice(zl * 8, zl * 8 + 8)
        for zh in range(2):
            place = zh * ZL + zl
            out[place, :, :D] = jnp.concatenate([part_in[at], part_grad[at]], axis=0).astype(bf16)
            out[place, :, D:] = jnp.concatenate([stats[at], stats[at]], axis=0).astype(bf16)


def middle_kernel(where_am_i, got, out, kept, stats_out):
    halves = [got[h * ZL : (h + 1) * ZL].reshape(LANES, WIDE).astype(f32) for h in range(2)]
    weighed = (lax.broadcasted_iota(jnp.int32, (LANES, 1), 0) & 8) == 0
    summed, top, total = merged(weighed, halves)
    kept[...] = summed
    stats_out[...] = lanes_of([top, total])
    row = lax.broadcasted_iota(jnp.int32, (LANES, LANES), 0)
    col = lax.broadcasted_iota(jnp.int32, (LANES, LANES), 1)
    source = (row & 7) * 16 + (row & 8) + (row >> 4)
    pick = jnp.where(col == source, 1.0, 0.0).astype(bf16)
    sorted_rows = jnp.dot(pick, summed.astype(bf16), preferred_element_type=f32).astype(bf16)
    for yx in range(Y * XH):
        for xl in range(2):
            out[2 * yx + xl] = sorted_rows[yx * 16 : yx * 16 + 16]


def array_rows(ref, array):
    return ref[:, array].astype(f32).reshape(LANES, D).astype(bf16)


def expert_kernel(where_am_i, rows, up_own, up_other, down_own, down_other, out, pre_grads, hiddens):
    slot_in, slot_grad = array_rows(rows, 0), array_rows(rows, 1)
    in_grad = jnp.zeros((LANES, D), f32)
    slot_out = jnp.zeros((LANES, D), f32)
    for j, (w_up, w_down) in enumerate(((up_own, down_own), (up_other, down_other))):
        pre_act = lax.dot_general(w_up[...], slot_in, NT, preferred_element_type=f32)
        hid_grad = lax.dot_general(w_down[...], slot_grad, NT, preferred_element_type=f32)
        cdf = 0.5 * (1.0 + lax.erf(pre_act * 0.7071067811865476))
        density = jnp.exp(pre_act * pre_act * -0.5) * 0.3989422804014327
        hiddens[j] = (pre_act * cdf).astype(bf16)
        pre_grads[j] = (hid_grad * (cdf + pre_act * density)).astype(bf16)
        in_grad += lax.dot_general(pre_grads[j], w_up[...], TN, preferred_element_type=f32)
        slot_out += lax.dot_general(hiddens[j], w_down[...], TN, preferred_element_type=f32)
    out[:, 0] = in_grad.reshape(16, 8, D).astype(bf16)
    out[:, 1] = slot_out.reshape(16, 8, D).astype(bf16)


def weights_kernel(where_am_i, pre_grads, hiddens, rows, keep, send):
    slot_in, slot_grad = array_rows(rows, 0), array_rows(rows, 1)
    for j, out in enumerate((keep, send)):
        out[0] = jnp.dot(pre_grads[j], slot_in, preferred_element_type=f32).astype(bf16)
        out[1] = jnp.dot(hiddens[j], slot_grad, preferred_element_type=f32).astype(bf16)


def return_kernel(where_am_i, got, kept, stats, out):
    row = lax.broadcasted_iota(jnp.int32, (LANES, 2 * LANES), 0)
    col = lax.broadcasted_iota(jnp.int32, (LANES, 2 * LANES), 1)
    source = (row & 7) * 32 + (row & 8) + (row >> 4)
    pick = jnp.where((col & ~16) == source, 1.0, 0.0).astype(bf16)
    summed = jnp.dot(pick, got[...], preferred_element_type=f32).astype(bf16)
    share = jnp.sum(kept[...] * summed.astype(f32), axis=1, keepdims=True)
    top, total = stats[:, 0:1], stats[:, 1:2]
    extra = lanes_of(pieces(share) + pieces(top) + pieces(total)).astype(bf16)
    for zl in range(ZL):
        at = slice(zl * 16, zl * 16 + 16)
        for zh in range(2):
            out[zh * ZL + zl, :, :D] = summed[at]
            out[zh * ZL + zl, :, D:] = extra[at]


def tokens_kernel(
    where_am_i, router_hbm, tok_a, tok_b, grad_a, grad_b, got_hbm, own_grad, sent_grad, router_grad,
    router_t, tok, grad, got, arrived,
):
    core = where_am_i[0]
    own, other = pl.ds(0, 64), pl.ds(64, 64)
    moves = (
        (router_hbm, router_t),
        (tok_a.at[core], tok.at[own]),
        (tok_b.at[core], tok.at[other]),
        (got_hbm, got),
        (grad_a.at[core], grad.at[own]),
        (grad_b.at[core], grad.at[other]),
    )
    copies = [pltpu.make_async_copy(source, target, arrived.at[k]) for k, (source, target) in enumerate(moves)]
    for copy in copies:
        copy.start()
    for copy in copies:
        copy.wait()
    halves = [got[h * ZL : (h + 1) * ZL].astype(f32) for h in range(2)]
    both = halves[0] + halves[1]
    slot_in_grad = both[:, :8, :D].reshape(SLOTS, D).astype(bf16)
    slot_out = both[:, 8:, :D].reshape(SLOTS, D).astype(bf16)
    weighted = three(both[:, :8, D:].reshape(SLOTS, LANES), 0)
    stats = halves[0][:, :8, D:].reshape(SLOTS, LANES)
    top, total = three(stats, 3), three(stats, 6)
    logits = lax.dot_general(router_t[...], tok[...], NT, preferred_element_type=f32)
    dispatch = jnp.exp(logits - top) / total
    combine = combine_of(logits)
    cgrad = lax.dot_general(slot_out, grad[...], NT, preferred_element_type=f32)
    dgrad = lax.dot_general(slot_in_grad, tok[...], NT, preferred_element_type=f32)
    comb_part = combine * (cgrad - jnp.sum(combine * cgrad, axis=0, keepdims=True))
    disp_part = dispatch * (dgrad - weighted)
    logit_grad = (comb_part + disp_part).astype(bf16)
    by_expert = jnp.dot(slot_order(transpose=True), logit_grad, preferred_element_type=f32).astype(bf16)
    router_grad[...] = jnp.dot(by_expert, tok[...], preferred_element_type=f32).astype(bf16)
    left = jnp.concatenate([dispatch.astype(bf16), logit_grad], axis=0)
    right = jnp.concatenate([slot_in_grad, router_t[...]], axis=0)
    all_grad = lax.dot_general(left, right, TN, preferred_element_type=f32).astype(bf16)
    own_grad[...] = all_grad[:64]
    sent_grad[...] = all_grad[64:]


def swap(value):
    return lax.ppermute(value, "core", [(0, 1), (1, 0)])


def exchange(value, axes):
    return lax.all_to_all(value, axes, split_axis=0, concat_axis=0, tiled=True)


def on_device(tokens, router, up_proj, down_proj, out_grad):
    here = lax.axis_index("core").astype(jnp.int32).reshape(1)
    tok_b, grad_b = swap(tokens), swap(out_grad)
    slots, router_t = call(
        slots_kernel,
        [shaped((16, 16, WIDE), bf16), shaped((SLOTS, D), bf16)],
        here, router.T, tokens, tok_b, out_grad, grad_b,
    )
    got = exchange(slots, COLUMN)
    up_other, down_other = swap(up_proj[0]), swap(down_proj[0])
    by_expert, kept, stats = call(
        middle_kernel,
        [shaped((16, 16, D), bf16), shaped((LANES, D), f32), shaped((LANES, LANES), f32)],
        here, got, after=(up_other, down_other),
    )
    rows = exchange(by_expert.reshape(16, 2, 8, D), PLANE)
    done, pre_grads, hiddens = call(
        expert_kernel,
        [shaped((16, 2, 8, D), bf16), shaped((2, 320, LANES), bf16), shaped((2, 320, LANES), bf16)],
        here, rows, up_proj[0], up_other, down_proj[0], down_other,
    )
    back = exchange(done, PLANE).reshape(256, D)
    keep, send = call(
        weights_kernel, [shaped((2, 320, D), bf16), shaped((2, 320, D), bf16)], here, pre_grads, hiddens, rows
    )
    summed = (keep.astype(f32) + swap(send).astype(f32)).astype(bf16)
    (by_owner,) = call(return_kernel, [shaped((16, 16, WIDE), bf16)], here, back, kept, stats)
    got = exchange(by_owner, COLUMN)
    own_grad, sent_grad, router_part = pl.pallas_call(
        tokens_kernel,
        out_shape=[shaped((64, D), bf16), shaped((64, D), bf16), shaped((SLOTS, D), bf16)],
        in_specs=[SMEM] + [HBM] * 6,
        out_specs=[VMEM] * 3,
        scratch_shapes=[
            pltpu.VMEM((SLOTS, D), bf16),
            pltpu.VMEM((LANES, D), bf16),
            pltpu.VMEM((LANES, D), bf16),
            pltpu.VMEM((16, 16, WIDE), bf16),
            pltpu.SemaphoreType.DMA((6,)),
        ],
        compiler_params=pltpu.CompilerParams(vmem_limit_bytes=63 * 1024 * 1024),
    )(here, router_t, tokens, tok_b, out_grad, grad_b, got)
    got_grad = swap(sent_grad)
    own_first = here[0] == 0
    tokens_grad = jnp.where(own_first, jnp.stack([own_grad, got_grad]), jnp.stack([got_grad, own_grad]))
    part = exchange(router_part.reshape(32, 2, D), PLANE_CORES).astype(f32).sum(axis=0).astype(bf16)
    whole = exchange(jnp.broadcast_to(part, (16, 2, D)), COLUMN).astype(f32).sum(axis=0).astype(bf16)
    full = exchange(jnp.broadcast_to(whole, (32, 2, D)), PLANE_CORES).reshape(SLOTS, D)
    return tokens_grad, full.T.astype(f32), summed[:1], summed[1:]


def solution(mesh):
    fine = Mesh(mesh.devices.reshape(2, 2, Y, ZL, XH, 2), ("zh", "core", "y", "zl", "xh", "xl"))
    rows = P(EVERY_GROUP, ("zh", "core"), None)
    return jax.shard_map(
        on_device,
        mesh=fine,
        in_specs=(rows, P(), rows, rows, rows),
        out_specs=(rows, P(), rows, rows),
        check_vma=False,
    )
```

```python
import jax
import jax.numpy as jnp
from jax import lax
from jax.experimental import pallas as pl
from jax.experimental.pallas import tpu as pltpu
from jax.sharding import Mesh, PartitionSpec as P

D = 1280
LANES = 128
WIDE = D + LANES
SLOTS = 64
Y, ZL, XH = 4, 8, 2
PLANE = ("y", "xh", "xl")
PLANE_CORES = ("core", "y", "xh", "xl")
COLUMN = ("zh", "zl")
EVERY_GROUP = ("y", "zl", "xh", "xl")
bf16, f32 = jnp.bfloat16, jnp.float32
NT = (((1,), (1,)), ((), ()))
TN = (((0,), (0,)), ((), ()))
SMEM = pl.BlockSpec(memory_space=pltpu.SMEM)
VMEM = pl.BlockSpec(memory_space=pltpu.VMEM)
ANY = pl.BlockSpec(memory_space=pl.ANY)


def call(kernel, outs, *operands, after=()):
    body = kernel
    if after:
        first, last = len(operands), len(operands) + len(after)
        body = lambda *refs: kernel(*refs[:first], *refs[last:])
    bytes_accessed = sum(a.size * a.dtype.itemsize for a in list(operands) + list(outs))
    return pl.pallas_call(
        body,
        out_shape=outs,
        in_specs=[SMEM] + [VMEM] * (len(operands) - 1) + [ANY] * len(after),
        out_specs=[VMEM] * len(outs),
        compiler_params=pltpu.CompilerParams(vmem_limit_bytes=14 * 1024 * 1024),
        cost_estimate=pl.CostEstimate(flops=0, bytes_accessed=bytes_accessed, transcendentals=0),
    )(*operands, *after)


def shaped(shape, dtype):
    return jax.ShapeDtypeStruct(shape, dtype)


def pieces(value):
    first = value.astype(bf16).astype(f32)
    second = (value - first).astype(bf16).astype(f32)
    third = (value - first - second).astype(bf16).astype(f32)
    return [first, second, third]


def lanes_of(columns):
    rows = columns[0].shape[0]
    lane = lax.broadcasted_iota(jnp.int32, (rows, LANES), 1)
    packed = jnp.zeros((rows, LANES), f32)
    for k, column in enumerate(columns):
        packed = jnp.where(lane == k, column, packed)
    return packed


def three(stats, first):
    return stats[:, first : first + 1] + stats[:, first + 1 : first + 2] + stats[:, first + 2 : first + 3]


def combine_of(logits):
    raised = jnp.exp(logits - jnp.max(logits, axis=0, keepdims=True))
    return raised / jnp.sum(raised, axis=0, keepdims=True)


def slot_order(transpose=False):
    own = lax.broadcasted_iota(jnp.int32, (SLOTS, SLOTS), 1 if transpose else 0)
    expert = lax.broadcasted_iota(jnp.int32, (SLOTS, SLOTS), 0 if transpose else 1)
    return jnp.where(expert == ((own >> 1) & 3) * 16 + (own >> 3) * 2 + (own & 1), 1.0, 0.0).astype(bf16)


def merged(on_first, halves):
    tops = [three(h[:, D:], 0) for h in halves]
    totals = [three(h[:, D:], 3) for h in halves]
    top = jnp.maximum(tops[0], tops[1])
    parts = [totals[h] * jnp.exp(tops[h] - top) for h in range(2)]
    total = parts[0] + parts[1]
    shares = [jnp.where(on_first, part / total, 1.0) for part in parts]
    return halves[0][:, :D] * shares[0] + halves[1][:, :D] * shares[1], top, total


def slots_kernel(where_am_i, router_t, tok_own, tok_b, grad_own, grad_b, out):
    core = where_am_i[0]
    tok = jnp.concatenate([tok_own[...], tok_b[core]], axis=0)
    grad = jnp.concatenate([grad_own[...], grad_b[core]], axis=0)
    logits = lax.dot_general(router_t[...], tok, NT, preferred_element_type=f32)
    top = jnp.max(logits, axis=1, keepdims=True)
    raised = jnp.exp(logits - top)
    total = jnp.sum(raised, axis=1, keepdims=True)
    stats = lanes_of(pieces(top) + pieces(total))
    part_in = jnp.dot((raised / total).astype(bf16), tok, preferred_element_type=f32)
    part_grad = jnp.dot(combine_of(logits).astype(bf16), grad, preferred_element_type=f32)
    for zl in range(ZL):
        at = slice(zl * 8, zl * 8 + 8)
        for zh in range(2):
            place = zh * ZL + zl
            out[place, :, :D] = jnp.concatenate([part_in[at], part_grad[at]], axis=0).astype(bf16)
            out[place, :, D:] = jnp.concatenate([stats[at], stats[at]], axis=0).astype(bf16)


def middle_kernel(where_am_i, got, out, kept, stats_out):
    halves = [got[h * ZL : (h + 1) * ZL].reshape(LANES, WIDE).astype(f32) for h in range(2)]
    weighed = (lax.broadcasted_iota(jnp.int32, (LANES, 1), 0) & 8) == 0
    summed, top, total = merged(weighed, halves)
    kept[...] = summed
    stats_out[...] = lanes_of([top, total])
    row = lax.broadcasted_iota(jnp.int32, (LANES, LANES), 0)
    col = lax.broadcasted_iota(jnp.int32, (LANES, LANES), 1)
    source = (row & 7) * 16 + (row & 8) + (row >> 4)
    pick = jnp.where(col == source, 1.0, 0.0).astype(bf16)
    sorted_rows = jnp.dot(pick, summed.astype(bf16), preferred_element_type=f32).astype(bf16)
    for yx in range(Y * XH):
        for xl in range(2):
            out[2 * yx + xl] = sorted_rows[yx * 16 : yx * 16 + 16]


def array_rows(ref, array):
    return ref[:, array].astype(f32).reshape(LANES, D).astype(bf16)


def expert_kernel(where_am_i, rows, up_own, up_other, down_own, down_other, out, pre_grads, hiddens):
    slot_in, slot_grad = array_rows(rows, 0), array_rows(rows, 1)
    in_grad = jnp.zeros((LANES, D), f32)
    slot_out = jnp.zeros((LANES, D), f32)
    for j, (w_up, w_down) in enumerate(((up_own, down_own), (up_other, down_other))):
        pre_act = lax.dot_general(w_up[...], slot_in, NT, preferred_element_type=f32)
        hid_grad = lax.dot_general(w_down[...], slot_grad, NT, preferred_element_type=f32)
        cdf = 0.5 * (1.0 + lax.erf(pre_act * 0.7071067811865476))
        density = jnp.exp(pre_act * pre_act * -0.5) * 0.3989422804014327
        hiddens[j] = (pre_act * cdf).astype(bf16)
        pre_grads[j] = (hid_grad * (cdf + pre_act * density)).astype(bf16)
        in_grad += lax.dot_general(pre_grads[j], w_up[...], TN, preferred_element_type=f32)
        slot_out += lax.dot_general(hiddens[j], w_down[...], TN, preferred_element_type=f32)
    out[:, 0] = in_grad.reshape(16, 8, D).astype(bf16)
    out[:, 1] = slot_out.reshape(16, 8, D).astype(bf16)


def weights_kernel(where_am_i, pre_grads, hiddens, rows, keep, send):
    slot_in, slot_grad = array_rows(rows, 0), array_rows(rows, 1)
    for j, out in enumerate((keep, send)):
        out[0] = jnp.dot(pre_grads[j], slot_in, preferred_element_type=f32).astype(bf16)
        out[1] = jnp.dot(hiddens[j], slot_grad, preferred_element_type=f32).astype(bf16)


def return_kernel(where_am_i, got, kept, stats, tok_own, tok_b, grad_own, grad_b, out, tok, grad):
    core = where_am_i[0]
    tok[:64], tok[64:] = tok_own[...], tok_b[core]
    grad[:64], grad[64:] = grad_own[...], grad_b[core]
    row = lax.broadcasted_iota(jnp.int32, (LANES, 2 * LANES), 0)
    col = lax.broadcasted_iota(jnp.int32, (LANES, 2 * LANES), 1)
    source = (row & 7) * 32 + (row & 8) + (row >> 4)
    pick = jnp.where((col & ~16) == source, 1.0, 0.0).astype(bf16)
    summed = jnp.dot(pick, got[...], preferred_element_type=f32).astype(bf16)
    share = jnp.sum(kept[...] * summed.astype(f32), axis=1, keepdims=True)
    top, total = stats[:, 0:1], stats[:, 1:2]
    extra = lanes_of(pieces(share) + pieces(top) + pieces(total)).astype(bf16)
    for zl in range(ZL):
        at = slice(zl * 16, zl * 16 + 16)
        for zh in range(2):
            out[zh * ZL + zl, :, :D] = summed[at]
            out[zh * ZL + zl, :, D:] = extra[at]


def tokens_kernel(where_am_i, router_t, tok, grad, got, router_grad, left, right):
    halves = [got[h * ZL : (h + 1) * ZL].astype(f32) for h in range(2)]
    both = halves[0] + halves[1]
    slot_in_grad = both[:, :8, :D].reshape(SLOTS, D).astype(bf16)
    slot_out = both[:, 8:, :D].reshape(SLOTS, D).astype(bf16)
    weighted = three(both[:, :8, D:].reshape(SLOTS, LANES), 0)
    stats = halves[0][:, :8, D:].reshape(SLOTS, LANES)
    top, total = three(stats, 3), three(stats, 6)
    logits = lax.dot_general(router_t[...], tok[...], NT, preferred_element_type=f32)
    dispatch = jnp.exp(logits - top) / total
    combine = combine_of(logits)
    cgrad = lax.dot_general(slot_out, grad[...], NT, preferred_element_type=f32)
    dgrad = lax.dot_general(slot_in_grad, tok[...], NT, preferred_element_type=f32)
    comb_part = combine * (cgrad - jnp.sum(combine * cgrad, axis=0, keepdims=True))
    disp_part = dispatch * (dgrad - weighted)
    logit_grad = (comb_part + disp_part).astype(bf16)
    by_expert = jnp.dot(slot_order(transpose=True), logit_grad, preferred_element_type=f32).astype(bf16)
    rows = jnp.dot(by_expert, tok[...], preferred_element_type=f32).astype(bf16)
    for k in range(SLOTS // 2):
        router_grad[k] = rows[2 * k : 2 * k + 2]
    left[:SLOTS], left[SLOTS:] = dispatch.astype(bf16), logit_grad
    right[...] = slot_in_grad


def tokens_grad_kernel(where_am_i, left, right, router_t, own_grad, sent_grad):
    both = jnp.concatenate([right[...], router_t[...]], axis=0)
    all_grad = lax.dot_general(left[...], both, TN, preferred_element_type=f32).astype(bf16)
    own_grad[...] = all_grad[:64]
    sent_grad[...] = all_grad[64:]


def spread_kernel(where_am_i, got, out):
    summed = jnp.sum(got[...].astype(f32), axis=0).astype(bf16)
    for k in range(out.shape[0]):
        out[k] = summed


def swap(value):
    return lax.ppermute(value, "core", [(0, 1), (1, 0)])


def exchange(value, axes):
    return lax.all_to_all(value, axes, split_axis=0, concat_axis=0, tiled=True)


def on_device(tokens, router, up_proj, down_proj, out_grad):
    here = lax.axis_index("core").astype(jnp.int32).reshape(1)
    tok_b, grad_b = swap(tokens), swap(out_grad)
    on_first = here[0] == 0
    tok_own = jnp.where(on_first, tokens[0], tokens[1])
    grad_own = jnp.where(on_first, out_grad[0], out_grad[1])
    router_t = router.T.reshape(Y, ZL, XH, D).transpose(1, 0, 2, 3).reshape(SLOTS, D)
    (slots,) = call(
        slots_kernel, [shaped((16, 16, WIDE), bf16)], here, router_t, tok_own, tok_b, grad_own, grad_b
    )
    got = exchange(slots, COLUMN)
    up_other, down_other = swap(up_proj[0]), swap(down_proj[0])
    by_expert, kept, stats = call(
        middle_kernel,
        [shaped((16, 16, D), bf16), shaped((LANES, D), f32), shaped((LANES, LANES), f32)],
        here, got, after=(up_other, down_other),
    )
    rows = exchange(by_expert.reshape(16, 2, 8, D), PLANE)
    done, pre_grads, hiddens = call(
        expert_kernel,
        [shaped((16, 2, 8, D), bf16), shaped((2, 320, LANES), bf16), shaped((2, 320, LANES), bf16)],
        here, rows, up_proj[0], up_other, down_proj[0], down_other,
    )
    back = exchange(done, PLANE).reshape(256, D)
    keep, send = call(
        weights_kernel, [shaped((2, 320, D), bf16), shaped((2, 320, D), bf16)], here, pre_grads, hiddens, rows
    )
    got_send = swap(send)
    up_grad, down_grad = ((keep[k : k + 1].astype(f32) + got_send[k : k + 1].astype(f32)).astype(bf16) for k in range(2))
    by_owner, tok, grad = call(
        return_kernel,
        [shaped((16, 16, WIDE), bf16), shaped((LANES, D), bf16), shaped((LANES, D), bf16)],
        here, back, kept, stats, tok_own, tok_b, grad_own, grad_b,
    )
    got = exchange(by_owner, COLUMN)
    router_part, left, right = call(
        tokens_kernel,
        [shaped((32, 2, D), bf16), shaped((LANES, LANES), bf16), shaped((SLOTS, D), bf16)],
        here, router_t, tok, grad, got, after=(up_grad, down_grad),
    )
    own_grad, sent_grad = call(
        tokens_grad_kernel, [shaped((64, D), bf16), shaped((64, D), bf16)], here, left, right, router_t
    )
    got_grad = swap(sent_grad)
    (part,) = call(
        spread_kernel, [shaped((16, 2, D), bf16)], here, exchange(router_part, PLANE_CORES), after=(sent_grad,)
    )
    (whole,) = call(spread_kernel, [shaped((32, 2, D), bf16)], here, exchange(part, COLUMN))
    full = exchange(whole, PLANE_CORES).reshape(SLOTS, D)
    tokens_grad = jnp.where(on_first, jnp.stack([own_grad, got_grad]), jnp.stack([got_grad, own_grad]))
    return tokens_grad, full.T.astype(f32), up_grad, down_grad


def solution(mesh):
    fine = Mesh(mesh.devices.reshape(2, 2, Y, ZL, XH, 2), ("zh", "core", "y", "zl", "xh", "xl"))
    rows = P(EVERY_GROUP, ("zh", "core"), None)
    return jax.shard_map(
        on_device,
        mesh=fine,
        in_specs=(rows, P(), rows, rows, rows),
        out_specs=(rows, P(), rows, rows),
        check_vma=False,
    )
```

```python
import jax
import jax.numpy as jnp
import numpy as np
from jax import lax
from jax.experimental import pallas as pl
from jax.experimental.pallas import tpu as pltpu
from jax.sharding import Mesh, PartitionSpec as P

D = 1280
LANES = 128
WIDE = D + LANES
SLOTS = 64
Y, ZL, XH = 4, 8, 2
PLANE = ("y", "xh", "xl")
PLANE_CORES = ("core", "y", "xh", "xl")
COLUMN = ("zh", "zl")
ALL = ("zh", "core", "y", "zl", "xh", "xl")
EVERY_GROUP = ("y", "zl", "xh", "xl")
bf16, f32 = jnp.bfloat16, jnp.float32
NT = (((1,), (1,)), ((), ()))
TN = (((0,), (0,)), ((), ()))
SMEM = pl.BlockSpec(memory_space=pltpu.SMEM)
VMEM = pl.BlockSpec(memory_space=pltpu.VMEM)
ANY = pl.BlockSpec(memory_space=pl.ANY)


def call(kernel, outs, *operands, after=()):
    body = kernel
    if after:
        first, last = len(operands), len(operands) + len(after)
        body = lambda *refs: kernel(*refs[:first], *refs[last:])
    bytes_accessed = sum(a.size * a.dtype.itemsize for a in list(operands) + list(outs))
    return pl.pallas_call(
        body,
        out_shape=outs,
        in_specs=[SMEM] + [VMEM] * (len(operands) - 1) + [ANY] * len(after),
        out_specs=[VMEM] * len(outs),
        compiler_params=pltpu.CompilerParams(vmem_limit_bytes=20 * 1024 * 1024),
        cost_estimate=pl.CostEstimate(flops=0, bytes_accessed=bytes_accessed, transcendentals=0),
    )(*operands, *after)


def shaped(shape, dtype):
    return jax.ShapeDtypeStruct(shape, dtype)


def pieces(value):
    first = value.astype(bf16).astype(f32)
    second = (value - first).astype(bf16).astype(f32)
    third = (value - first - second).astype(bf16).astype(f32)
    return [first, second, third]


def lanes_of(columns):
    rows = columns[0].shape[0]
    lane = lax.broadcasted_iota(jnp.int32, (rows, LANES), 1)
    packed = jnp.zeros((rows, LANES), f32)
    for k, column in enumerate(columns):
        packed = jnp.where(lane == k, column, packed)
    return packed


def three(stats, first):
    return stats[:, first : first + 1] + stats[:, first + 1 : first + 2] + stats[:, first + 2 : first + 3]


def combine_of(logits):
    raised = jnp.exp(logits - jnp.max(logits, axis=0, keepdims=True))
    return raised / jnp.sum(raised, axis=0, keepdims=True)


def slot_order(transpose=False):
    own = lax.broadcasted_iota(jnp.int32, (SLOTS, SLOTS), 1 if transpose else 0)
    expert = lax.broadcasted_iota(jnp.int32, (SLOTS, SLOTS), 0 if transpose else 1)
    return jnp.where(expert == ((own >> 1) & 3) * 16 + (own >> 3) * 2 + (own & 1), 1.0, 0.0).astype(bf16)


def merged(on_first, halves):
    tops = [three(h[:, D:], 0) for h in halves]
    totals = [three(h[:, D:], 3) for h in halves]
    top = jnp.maximum(tops[0], tops[1])
    parts = [totals[h] * jnp.exp(tops[h] - top) for h in range(2)]
    total = parts[0] + parts[1]
    shares = [jnp.where(on_first, part / total, 1.0) for part in parts]
    return halves[0][:, :D] * shares[0] + halves[1][:, :D] * shares[1], top, total


def slots_kernel(where_am_i, router_t, tok_own, tok_b, grad_own, grad_b, out):
    core = where_am_i[0]
    tok = jnp.concatenate([tok_own[...], tok_b[core]], axis=0)
    grad = jnp.concatenate([grad_own[...], grad_b[core]], axis=0)
    logits = lax.dot_general(router_t[...], tok, NT, preferred_element_type=f32)
    top = jnp.max(logits, axis=1, keepdims=True)
    raised = jnp.exp(logits - top)
    total = jnp.sum(raised, axis=1, keepdims=True)
    stats = lanes_of(pieces(top) + pieces(total))
    part_in = jnp.dot((raised / total).astype(bf16), tok, preferred_element_type=f32)
    part_grad = jnp.dot(combine_of(logits).astype(bf16), grad, preferred_element_type=f32)
    for zl in range(ZL):
        at = slice(zl * 8, zl * 8 + 8)
        for zh in range(2):
            place = zh * ZL + zl
            out[place, 0, :, :D] = part_in[at].astype(bf16)
            out[place, 1, :, :D] = part_grad[at].astype(bf16)
            out[place, 0, :, D:] = stats[at].astype(bf16)
            out[place, 1, :, D:] = stats[at].astype(bf16)


def middle(got, out, kept, stats_out):
    halves = [got[h * ZL : (h + 1) * ZL].astype(f32).reshape(LANES, WIDE) for h in range(2)]
    weighed = (lax.broadcasted_iota(jnp.int32, (LANES, 1), 0) & 8) == 0
    summed, top, total = merged(weighed, halves)
    kept[...] = summed
    stats_out[...] = lanes_of([top, total])
    row = lax.broadcasted_iota(jnp.int32, (LANES, LANES), 0)
    col = lax.broadcasted_iota(jnp.int32, (LANES, LANES), 1)
    source = (row & 7) * 16 + (row & 8) + (row >> 4)
    pick = jnp.where(col == source, 1.0, 0.0).astype(bf16)
    sorted_rows = jnp.dot(pick, summed.astype(bf16), preferred_element_type=f32)
    for yx in range(Y * XH):
        for array in range(2):
            at = yx * 16 + array * 8
            for xl in range(2):
                out[2 * yx + xl, array, :, :D] = sorted_rows[at : at + 8].astype(bf16)


def array_rows(ref, array):
    return ref[:, array, :, :D].astype(f32).reshape(LANES, D).astype(bf16)


def expert(rows, up_own, up_other, down_own, down_other, out, pre_grads, hiddens):
    slot_in, slot_grad = array_rows(rows, 0), array_rows(rows, 1)
    in_grad = jnp.zeros((LANES, D), f32)
    slot_out = jnp.zeros((LANES, D), f32)
    for j, (w_up, w_down) in enumerate(((up_own, down_own), (up_other, down_other))):
        pre_act = lax.dot_general(w_up[...], slot_in, NT, preferred_element_type=f32)
        hid_grad = lax.dot_general(w_down[...], slot_grad, NT, preferred_element_type=f32)
        cdf = 0.5 * (1.0 + lax.erf(pre_act * 0.7071067811865476))
        density = jnp.exp(pre_act * pre_act * -0.5) * 0.3989422804014327
        hiddens[j] = (pre_act * cdf).astype(bf16)
        pre_grads[j] = (hid_grad * (cdf + pre_act * density)).astype(bf16)
        in_grad += lax.dot_general(pre_grads[j], w_up[...], TN, preferred_element_type=f32)
        slot_out += lax.dot_general(hiddens[j], w_down[...], TN, preferred_element_type=f32)
    out[:, 0, :, :D] = in_grad.reshape(16, 8, D).astype(bf16)
    out[:, 1, :, :D] = slot_out.reshape(16, 8, D).astype(bf16)


def weight_grads(pre_grads, hiddens, rows, keep, send):
    slot_in, slot_grad = array_rows(rows, 0), array_rows(rows, 1)
    for j, out in enumerate((keep, send)):
        out[0] = jnp.dot(pre_grads[j], slot_in, preferred_element_type=f32).astype(bf16)
        out[1] = jnp.dot(hiddens[j], slot_grad, preferred_element_type=f32).astype(bf16)


def back_to_owners(got, kept, stats, out):
    row = lax.broadcasted_iota(jnp.int32, (LANES, 2 * LANES), 0)
    col = lax.broadcasted_iota(jnp.int32, (LANES, 2 * LANES), 1)
    source = (row & 7) * 32 + (row & 8) + (row >> 4)
    pick = jnp.where((col & ~16) == source, 1.0, 0.0).astype(bf16)
    rows = got[:, :, :, :D].astype(f32).reshape(2 * LANES, D).astype(bf16)
    summed = jnp.dot(pick, rows, preferred_element_type=f32).astype(bf16).astype(f32)
    share = jnp.sum(kept[...] * summed, axis=1, keepdims=True)
    top, total = stats[:, 0:1], stats[:, 1:2]
    extra = lanes_of(pieces(share) + pieces(top) + pieces(total))
    for zl in range(ZL):
        for array in range(2):
            at = slice(zl * 16 + array * 8, zl * 16 + array * 8 + 8)
            for zh in range(2):
                out[zh * ZL + zl, array, :, :D] = summed[at].astype(bf16)
                out[zh * ZL + zl, array, :, D:] = extra[at].astype(bf16)


def phase_2(where_am_i, got, slots, out, kept, stats):
    @pl.when(where_am_i[0] == 1)
    def _():
        middle(got, out, kept, stats)

    @pl.when(where_am_i[0] == 0)
    def _():
        out[...] = slots[...]


def phase_3(where_am_i, got, up_own, up_other, down_own, down_other, out, kept, stats, pre_grads, hiddens):
    @pl.when(where_am_i[0] == 1)
    def _():
        expert(got, up_own, up_other, down_own, down_other, out, pre_grads, hiddens)

    @pl.when(where_am_i[0] == 0)
    def _():
        middle(got, out, kept, stats)


def phase_4(where_am_i, got, kept, stats, up_own, up_other, down_own, down_other, out, pre_grads, hiddens):
    @pl.when(where_am_i[0] == 1)
    def _():
        back_to_owners(got, kept, stats, out)

    @pl.when(where_am_i[0] == 0)
    def _():
        expert(got, up_own, up_other, down_own, down_other, out, pre_grads, hiddens)


def phase_5(where_am_i, got, kept, stats, tok_own, tok_b, grad_own, grad_b, out, tok, grad):
    core = where_am_i[0]
    tok[:64], tok[64:] = tok_own[...], tok_b[core]
    grad[:64], grad[64:] = grad_own[...], grad_b[core]

    @pl.when(core == 0)
    def _():
        back_to_owners(got, kept, stats, out)

    @pl.when(core == 1)
    def _():
        out[...] = got[...]


def weights_kernel(where_am_i, pre_3, hid_3, rows_3, pre_4, hid_4, rows_4, keep, send):
    @pl.when(where_am_i[0] == 1)
    def _():
        weight_grads(pre_3, hid_3, rows_3, keep, send)

    @pl.when(where_am_i[0] == 0)
    def _():
        weight_grads(pre_4, hid_4, rows_4, keep, send)


def tokens_kernel(where_am_i, router_t, tok, grad, got_4, got_5, router_grad, left, right):
    spans = [slice(h * ZL, (h + 1) * ZL) for h in range(2)]
    halves = [jnp.where(where_am_i[0] == 1, got_4[span], got_5[span]).astype(f32) for span in spans]
    both = halves[0] + halves[1]
    slot_in_grad = both[:, 0, :, :D].reshape(SLOTS, D).astype(bf16)
    slot_out = both[:, 1, :, :D].reshape(SLOTS, D).astype(bf16)
    weighted = three(both[:, 0, :, D:].reshape(SLOTS, LANES), 0)
    stats = halves[0][:, 0, :, D:].reshape(SLOTS, LANES)
    top, total = three(stats, 3), three(stats, 6)
    logits = lax.dot_general(router_t[...], tok[...], NT, preferred_element_type=f32)
    dispatch = jnp.exp(logits - top) / total
    combine = combine_of(logits)
    cgrad = lax.dot_general(slot_out, grad[...], NT, preferred_element_type=f32)
    dgrad = lax.dot_general(slot_in_grad, tok[...], NT, preferred_element_type=f32)
    comb_part = combine * (cgrad - jnp.sum(combine * cgrad, axis=0, keepdims=True))
    disp_part = dispatch * (dgrad - weighted)
    logit_grad = (comb_part + disp_part).astype(bf16)
    by_expert = jnp.dot(slot_order(transpose=True), logit_grad, preferred_element_type=f32).astype(bf16)
    rows = jnp.dot(by_expert, tok[...], preferred_element_type=f32).astype(bf16)
    for k in range(SLOTS // 2):
        router_grad[k] = rows[2 * k : 2 * k + 2]
    left[:SLOTS], left[SLOTS:] = dispatch.astype(bf16), logit_grad
    right[...] = slot_in_grad


def tokens_grad_kernel(where_am_i, left, right, router_t, own_grad, sent_grad):
    both = jnp.concatenate([right[...], router_t[...]], axis=0)
    all_grad = lax.dot_general(left[...], both, TN, preferred_element_type=f32).astype(bf16)
    own_grad[...] = all_grad[:64]
    sent_grad[...] = all_grad[64:]


def spread_kernel(where_am_i, got, out):
    summed = jnp.sum(got[...].astype(f32), axis=0).astype(bf16)
    for k in range(out.shape[0]):
        out[k] = summed


def swap(value):
    return lax.ppermute(value, "core", [(0, 1), (1, 0)])


def exchange(value, axes):
    return lax.all_to_all(value, axes, split_axis=0, concat_axis=0, tiled=True)


def mixed(value, first_axes, second_axes):
    ids = np.arange(512).reshape(2, 2, Y, ZL, XH, 2)
    orders = {PLANE: (0, 2, 1, 3, 4), COLUMN: (1, 3, 4, 0, 2)}
    groups = [ids[:, core].transpose(orders[axes]).reshape(16, 16) for core, axes in enumerate((first_axes, second_axes))]
    return lax.all_to_all(
        value, ALL, split_axis=0, concat_axis=0, tiled=True, axis_index_groups=np.concatenate(groups).tolist()
    )


def on_device(tokens, router, up_proj, down_proj, out_grad):
    here = lax.axis_index("core").astype(jnp.int32).reshape(1)
    tok_b, grad_b = swap(tokens), swap(out_grad)
    on_first = here[0] == 0
    tok_own = jnp.where(on_first, tokens[0], tokens[1])
    grad_own = jnp.where(on_first, out_grad[0], out_grad[1])
    router_t = router.T.reshape(Y, ZL, XH, D).transpose(1, 0, 2, 3).reshape(SLOTS, D)
    wide = shaped((16, 2, 8, WIDE), bf16)
    acts = [shaped((2, 320, LANES), bf16)] * 2
    held = [shaped((LANES, D), f32), shaped((LANES, LANES), f32)]
    (slots,) = call(slots_kernel, [wide], here, router_t, tok_own, tok_b, grad_own, grad_b)
    got_1 = mixed(slots, PLANE, COLUMN)
    up_other, down_other = swap(up_proj[0]), swap(down_proj[0])
    weights = (up_proj[0], up_other, down_proj[0], down_other)
    sent_2, kept_1, stats_1 = call(phase_2, [wide, *held], here, got_1, slots, after=(up_other, down_other))
    got_2 = mixed(sent_2, COLUMN, PLANE)
    sent_3, kept_0, stats_0, pre_1, hid_1 = call(phase_3, [wide, *held, *acts], here, got_2, *weights)
    got_3 = exchange(sent_3, PLANE)
    sent_4, pre_0, hid_0 = call(phase_4, [wide, *acts], here, got_3, kept_1, stats_1, *weights)
    got_4 = mixed(sent_4, PLANE, COLUMN)
    keep, send = call(
        weights_kernel, [shaped((2, 320, D), bf16), shaped((2, 320, D), bf16)],
        here, pre_1, hid_1, got_2, pre_0, hid_0, got_3,
    )
    got_send = swap(send)
    up_grad, down_grad = ((keep[k : k + 1].astype(f32) + got_send[k : k + 1].astype(f32)).astype(bf16) for k in range(2))
    sent_5, tok, grad = call(
        phase_5, [wide, shaped((LANES, D), bf16), shaped((LANES, D), bf16)],
        here, got_4, kept_0, stats_0, tok_own, tok_b, grad_own, grad_b,
    )
    got_5 = mixed(sent_5, COLUMN, PLANE)
    router_part, left, right = call(
        tokens_kernel,
        [shaped((32, 2, D), bf16), shaped((LANES, LANES), bf16), shaped((SLOTS, D), bf16)],
        here, router_t, tok, grad, got_4, got_5, after=(up_grad, down_grad),
    )
    own_grad, sent_grad = call(
        tokens_grad_kernel, [shaped((64, D), bf16), shaped((64, D), bf16)], here, left, right, router_t
    )
    got_grad = swap(sent_grad)
    (part,) = call(
        spread_kernel, [shaped((16, 2, D), bf16)], here, exchange(router_part, PLANE_CORES), after=(sent_grad,)
    )
    (whole,) = call(spread_kernel, [shaped((32, 2, D), bf16)], here, exchange(part, COLUMN))
    full = exchange(whole, PLANE_CORES).reshape(SLOTS, D)
    tokens_grad = jnp.where(on_first, jnp.stack([own_grad, got_grad]), jnp.stack([got_grad, own_grad]))
    return tokens_grad, full.T.astype(f32), up_grad, down_grad


def solution(mesh):
    fine = Mesh(mesh.devices.reshape(2, 2, Y, ZL, XH, 2), ("zh", "core", "y", "zl", "xh", "xl"))
    rows = P(EVERY_GROUP, ("zh", "core"), None)
    return jax.shard_map(
        on_device,
        mesh=fine,
        in_specs=(rows, P(), rows, rows, rows),
        out_specs=(rows, P(), rows, rows),
        check_vma=False,
    )
```

```python
import jax
import jax.numpy as jnp
import numpy as np
from jax import lax
from jax.experimental import pallas as pl
from jax.experimental.pallas import tpu as pltpu
from jax.sharding import Mesh, PartitionSpec as P

D = 1280
LANES = 128
WIDE = D + LANES
SLOTS = 64
Y, ZL, XH = 4, 8, 2
PLANE = ("y", "xh", "xl")
PLANE_CORES = ("core", "y", "xh", "xl")
COLUMN = ("zh", "zl")
ALL = ("zh", "core", "y", "zl", "xh", "xl")
EVERY_GROUP = ("y", "zl", "xh", "xl")
bf16, f32 = jnp.bfloat16, jnp.float32
NT = (((1,), (1,)), ((), ()))
TN = (((0,), (0,)), ((), ()))
SMEM = pl.BlockSpec(memory_space=pltpu.SMEM)
VMEM = pl.BlockSpec(memory_space=pltpu.VMEM)
ANY = pl.BlockSpec(memory_space=pl.ANY)
HBM = pl.BlockSpec(memory_space=pltpu.HBM)


def call(kernel, outs, *operands, after=(), stored=(), after_spec=None):
    first, last = len(operands), len(operands) + len(after)
    body = (lambda *refs: kernel(*refs[:first], *refs[last:])) if after else kernel
    bytes_accessed = sum(a.size * a.dtype.itemsize for a in (*operands, *outs, *stored))
    return pl.pallas_call(
        body,
        out_shape=[*outs, *stored],
        in_specs=[SMEM] + [VMEM] * (len(operands) - 1) + [after_spec or ANY] * len(after),
        out_specs=[VMEM] * len(outs) + [HBM] * len(stored),
        scratch_shapes=[pltpu.VMEM(a.shape, a.dtype) for a in stored] + [pltpu.SemaphoreType.DMA(())] * len(stored),
        compiler_params=pltpu.CompilerParams(vmem_limit_bytes=20 * 1024 * 1024),
        cost_estimate=pl.CostEstimate(flops=0, bytes_accessed=bytes_accessed, transcendentals=0),
    )(*operands, *after)


def shaped(shape, dtype):
    return jax.ShapeDtypeStruct(shape, dtype)


def pieces(value):
    first = value.astype(bf16).astype(f32)
    second = (value - first).astype(bf16).astype(f32)
    third = (value - first - second).astype(bf16).astype(f32)
    return [first, second, third]


def lanes_of(columns):
    rows = columns[0].shape[0]
    lane = lax.broadcasted_iota(jnp.int32, (rows, LANES), 1)
    packed = jnp.zeros((rows, LANES), f32)
    for k, column in enumerate(columns):
        packed = jnp.where(lane == k, column, packed)
    return packed


def three(stats, first):
    return stats[:, first : first + 1] + stats[:, first + 1 : first + 2] + stats[:, first + 2 : first + 3]


def combine_of(logits):
    raised = jnp.exp(logits - jnp.max(logits, axis=0, keepdims=True))
    return raised / jnp.sum(raised, axis=0, keepdims=True)


def slot_order(transpose=False):
    own = lax.broadcasted_iota(jnp.int32, (SLOTS, SLOTS), 1 if transpose else 0)
    expert = lax.broadcasted_iota(jnp.int32, (SLOTS, SLOTS), 0 if transpose else 1)
    return jnp.where(expert == ((own >> 1) & 3) * 16 + (own >> 3) * 2 + (own & 1), 1.0, 0.0).astype(bf16)


def merged(on_first, halves):
    tops = [three(h[:, D:], 0) for h in halves]
    totals = [three(h[:, D:], 3) for h in halves]
    top = jnp.maximum(tops[0], tops[1])
    parts = [totals[h] * jnp.exp(tops[h] - top) for h in range(2)]
    total = parts[0] + parts[1]
    shares = [jnp.where(on_first, part / total, 1.0) for part in parts]
    return halves[0][:, :D] * shares[0] + halves[1][:, :D] * shares[1], top, total


def slots_kernel(where_am_i, router_t, tok_own, tok_b, grad_own, grad_b, out):
    core = where_am_i[0]
    tok = jnp.concatenate([tok_own[...], tok_b[core]], axis=0)
    grad = jnp.concatenate([grad_own[...], grad_b[core]], axis=0)
    logits = lax.dot_general(router_t[...], tok, NT, preferred_element_type=f32)
    top = jnp.max(logits, axis=1, keepdims=True)
    raised = jnp.exp(logits - top)
    total = jnp.sum(raised, axis=1, keepdims=True)
    stats = lanes_of(pieces(top) + pieces(total))
    part_in = jnp.dot((raised / total).astype(bf16), tok, preferred_element_type=f32)
    part_grad = jnp.dot(combine_of(logits).astype(bf16), grad, preferred_element_type=f32)
    for zl in range(ZL):
        at = slice(zl * 8, zl * 8 + 8)
        for zh in range(2):
            place = zh * ZL + zl
            out[place, 0, :, :D] = part_in[at].astype(bf16)
            out[place, 1, :, :D] = part_grad[at].astype(bf16)
            out[place, 0, :, D:] = stats[at].astype(bf16)
            out[place, 1, :, D:] = stats[at].astype(bf16)


def middle(got, out, kept, stats_out):
    halves = [got[h * ZL : (h + 1) * ZL].astype(f32).reshape(LANES, WIDE) for h in range(2)]
    weighed = (lax.broadcasted_iota(jnp.int32, (LANES, 1), 0) & 8) == 0
    summed, top, total = merged(weighed, halves)
    kept[...] = summed
    stats_out[...] = lanes_of([top, total])
    row = lax.broadcasted_iota(jnp.int32, (LANES, LANES), 0)
    col = lax.broadcasted_iota(jnp.int32, (LANES, LANES), 1)
    source = (row & 7) * 16 + (row & 8) + (row >> 4)
    pick = jnp.where(col == source, 1.0, 0.0).astype(bf16)
    sorted_rows = jnp.dot(pick, summed.astype(bf16), preferred_element_type=f32)
    for yx in range(Y * XH):
        for array in range(2):
            at = yx * 16 + array * 8
            for xl in range(2):
                out[2 * yx + xl, array, :, :D] = sorted_rows[at : at + 8].astype(bf16)


def array_rows(ref, array):
    return ref[:, array, :, :D].astype(f32).reshape(LANES, D).astype(bf16)


def expert(rows, up_own, up_other, down_own, down_other, out, pre_grads, hiddens):
    slot_in, slot_grad = array_rows(rows, 0), array_rows(rows, 1)
    in_grad = jnp.zeros((LANES, D), f32)
    slot_out = jnp.zeros((LANES, D), f32)
    for j, (w_up, w_down) in enumerate(((up_own, down_own), (up_other, down_other))):
        pre_act = lax.dot_general(w_up[...], slot_in, NT, preferred_element_type=f32)
        hid_grad = lax.dot_general(w_down[...], slot_grad, NT, preferred_element_type=f32)
        cdf = 0.5 * (1.0 + lax.erf(pre_act * 0.7071067811865476))
        density = jnp.exp(pre_act * pre_act * -0.5) * 0.3989422804014327
        hiddens[j] = (pre_act * cdf).astype(bf16)
        pre_grads[j] = (hid_grad * (cdf + pre_act * density)).astype(bf16)
        in_grad += lax.dot_general(pre_grads[j], w_up[...], TN, preferred_element_type=f32)
        slot_out += lax.dot_general(hiddens[j], w_down[...], TN, preferred_element_type=f32)
    out[:, 0, :, :D] = in_grad.reshape(16, 8, D).astype(bf16)
    out[:, 1, :, :D] = slot_out.reshape(16, 8, D).astype(bf16)


def weight_grads(pre_grads, hiddens, rows, keep, send):
    slot_in, slot_grad = array_rows(rows, 0), array_rows(rows, 1)
    for j, out in enumerate((keep, send)):
        out[0] = jnp.dot(pre_grads[j], slot_in, preferred_element_type=f32).astype(bf16)
        out[1] = jnp.dot(hiddens[j], slot_grad, preferred_element_type=f32).astype(bf16)


def back_to_owners(got, kept, stats, out):
    row = lax.broadcasted_iota(jnp.int32, (LANES, 2 * LANES), 0)
    col = lax.broadcasted_iota(jnp.int32, (LANES, 2 * LANES), 1)
    source = (row & 7) * 32 + (row & 8) + (row >> 4)
    pick = jnp.where((col & ~16) == source, 1.0, 0.0).astype(bf16)
    rows = got[:, :, :, :D].astype(f32).reshape(2 * LANES, D).astype(bf16)
    summed = jnp.dot(pick, rows, preferred_element_type=f32).astype(bf16).astype(f32)
    share = jnp.sum(kept[...] * summed, axis=1, keepdims=True)
    top, total = stats[:, 0:1], stats[:, 1:2]
    extra = lanes_of(pieces(share) + pieces(top) + pieces(total))
    for zl in range(ZL):
        for array in range(2):
            at = slice(zl * 16 + array * 8, zl * 16 + array * 8 + 8)
            for zh in range(2):
                out[zh * ZL + zl, array, :, :D] = summed[at].astype(bf16)
                out[zh * ZL + zl, array, :, D:] = extra[at].astype(bf16)


def phase_2(where_am_i, got, slots, out, kept, stats):
    @pl.when(where_am_i[0] == 1)
    def _():
        middle(got, out, kept, stats)

    @pl.when(where_am_i[0] == 0)
    def _():
        out[...] = slots[...]


def phase_3(where_am_i, got, up_own, up_other, down_own, down_other, out, kept, stats, pre_grads, hiddens):
    @pl.when(where_am_i[0] == 1)
    def _():
        expert(got, up_own, up_other, down_own, down_other, out, pre_grads, hiddens)

    @pl.when(where_am_i[0] == 0)
    def _():
        middle(got, out, kept, stats)


def phase_4(where_am_i, got, kept, stats, up_own, up_other, down_own, down_other, out, pre_grads, hiddens):
    @pl.when(where_am_i[0] == 1)
    def _():
        back_to_owners(got, kept, stats, out)

    @pl.when(where_am_i[0] == 0)
    def _():
        expert(got, up_own, up_other, down_own, down_other, out, pre_grads, hiddens)


def phase_5(
    where_am_i, got, kept, stats, tok_a, tok_b, grad_a, grad_b, out, tok_store, grad_store, tok, grad, *done
):
    core = where_am_i[0]
    tok[:64], tok[64:] = tok_a[core], tok_b[core]
    grad[:64], grad[64:] = grad_a[core], grad_b[core]
    copies = [
        pltpu.make_async_copy(source, target, done[k])
        for k, (source, target) in enumerate(((tok, tok_store), (grad, grad_store)))
    ]
    for copy in copies:
        copy.start()

    @pl.when(core == 0)
    def _():
        back_to_owners(got, kept, stats, out)

    @pl.when(core == 1)
    def _():
        out[...] = got[...]

    for copy in copies:
        copy.wait()


def weights_kernel(where_am_i, pre_3, hid_3, rows_3, pre_4, hid_4, rows_4, keep, send):
    @pl.when(where_am_i[0] == 1)
    def _():
        weight_grads(pre_3, hid_3, rows_3, keep, send)

    @pl.when(where_am_i[0] == 0)
    def _():
        weight_grads(pre_4, hid_4, rows_4, keep, send)


def tokens_kernel(where_am_i, router_t, tok, grad, got_4, got_5, router_grad, left, right):
    spans = [slice(h * ZL, (h + 1) * ZL) for h in range(2)]
    halves = [jnp.where(where_am_i[0] == 1, got_4[span], got_5[span]).astype(f32) for span in spans]
    both = halves[0] + halves[1]
    slot_in_grad = both[:, 0, :, :D].reshape(SLOTS, D).astype(bf16)
    slot_out = both[:, 1, :, :D].reshape(SLOTS, D).astype(bf16)
    weighted = three(both[:, 0, :, D:].reshape(SLOTS, LANES), 0)
    stats = halves[0][:, 0, :, D:].reshape(SLOTS, LANES)
    top, total = three(stats, 3), three(stats, 6)
    logits = lax.dot_general(router_t[...], tok[...], NT, preferred_element_type=f32)
    dispatch = jnp.exp(logits - top) / total
    combine = combine_of(logits)
    cgrad = lax.dot_general(slot_out, grad[...], NT, preferred_element_type=f32)
    dgrad = lax.dot_general(slot_in_grad, tok[...], NT, preferred_element_type=f32)
    comb_part = combine * (cgrad - jnp.sum(combine * cgrad, axis=0, keepdims=True))
    disp_part = dispatch * (dgrad - weighted)
    logit_grad = (comb_part + disp_part).astype(bf16)
    by_expert = jnp.dot(slot_order(transpose=True), logit_grad, preferred_element_type=f32).astype(bf16)
    rows = jnp.dot(by_expert, tok[...], preferred_element_type=f32).astype(bf16)
    for k in range(SLOTS // 2):
        router_grad[k] = rows[2 * k : 2 * k + 2]
    left[:SLOTS], left[SLOTS:] = dispatch.astype(bf16), logit_grad
    right[...] = slot_in_grad


def tokens_grad_kernel(where_am_i, left, right, router_t, own_grad, sent_grad):
    both = jnp.concatenate([right[...], router_t[...]], axis=0)
    all_grad = lax.dot_general(left[...], both, TN, preferred_element_type=f32).astype(bf16)
    own_grad[...] = all_grad[:64]
    sent_grad[...] = all_grad[64:]


def spread_kernel(where_am_i, got, out):
    summed = jnp.sum(got[...].astype(f32), axis=0).astype(bf16)
    for k in range(out.shape[0]):
        out[k] = summed


def swap(value):
    return lax.ppermute(value, "core", [(0, 1), (1, 0)])


def exchange(value, axes):
    return lax.all_to_all(value, axes, split_axis=0, concat_axis=0, tiled=True)


def mixed(value, first_axes, second_axes):
    ids = np.arange(512).reshape(2, 2, Y, ZL, XH, 2)
    orders = {PLANE: (0, 2, 1, 3, 4), COLUMN: (1, 3, 4, 0, 2)}
    groups = [ids[:, core].transpose(orders[axes]).reshape(16, 16) for core, axes in enumerate((first_axes, second_axes))]
    return lax.all_to_all(
        value, ALL, split_axis=0, concat_axis=0, tiled=True, axis_index_groups=np.concatenate(groups).tolist()
    )


def on_device(tokens, router, up_proj, down_proj, out_grad):
    here = lax.axis_index("core").astype(jnp.int32).reshape(1)
    tok_b, grad_b = swap(tokens), swap(out_grad)
    on_first = here[0] == 0
    tok_own = jnp.where(on_first, tokens[0], tokens[1])
    grad_own = jnp.where(on_first, out_grad[0], out_grad[1])
    router_t = router.T.reshape(Y, ZL, XH, D).transpose(1, 0, 2, 3).reshape(SLOTS, D)
    wide = shaped((16, 2, 8, WIDE), bf16)
    acts = [shaped((2, 320, LANES), bf16)] * 2
    held = [shaped((LANES, D), f32), shaped((LANES, LANES), f32)]
    (slots,) = call(slots_kernel, [wide], here, router_t, tok_own, tok_b, grad_own, grad_b)
    got_1 = mixed(slots, PLANE, COLUMN)
    up_other, down_other = swap(up_proj[0]), swap(down_proj[0])
    weights = (up_proj[0], up_other, down_proj[0], down_other)
    sent_2, kept_1, stats_1 = call(phase_2, [wide, *held], here, got_1, slots, after=weights, after_spec=VMEM)
    got_2 = mixed(sent_2, COLUMN, PLANE)
    sent_3, kept_0, stats_0, pre_1, hid_1 = call(phase_3, [shaped((16, 2, 8, D), bf16), *held, *acts], here, got_2, *weights)
    got_3 = exchange(sent_3, PLANE)
    sent_4, pre_0, hid_0 = call(phase_4, [wide, *acts], here, got_3, kept_1, stats_1, *weights)
    got_4 = mixed(sent_4, PLANE, COLUMN)
    keep, send = call(
        weights_kernel, [shaped((2, 320, D), bf16), shaped((2, 320, D), bf16)],
        here, pre_1, hid_1, got_2, pre_0, hid_0, got_3,
    )
    got_send = swap(send)
    up_grad, down_grad = ((keep[k : k + 1].astype(f32) + got_send[k : k + 1].astype(f32)).astype(bf16) for k in range(2))
    sent_5, tok, grad = call(
        phase_5, [wide], here, got_4, kept_0, stats_0, tokens, tok_b, out_grad, grad_b,
        stored=[shaped((LANES, D), bf16)] * 2,
    )
    got_5 = mixed(sent_5, COLUMN, PLANE)
    router_part, left, right = call(
        tokens_kernel,
        [shaped((32, 2, D), bf16), shaped((LANES, LANES), bf16), shaped((SLOTS, D), bf16)],
        here, router_t, tok, grad, got_4, got_5, after=(up_grad, down_grad),
    )
    own_grad, sent_grad = call(
        tokens_grad_kernel, [shaped((64, D), bf16), shaped((64, D), bf16)], here, left, right, router_t
    )
    got_grad = swap(sent_grad)
    (part,) = call(
        spread_kernel, [shaped((16, 2, D), bf16)], here, exchange(router_part, PLANE_CORES), after=(sent_grad,)
    )
    (whole,) = call(spread_kernel, [shaped((32, 2, D), bf16)], here, exchange(part, COLUMN))
    full = exchange(whole, PLANE_CORES).reshape(SLOTS, D)
    tokens_grad = jnp.where(on_first, jnp.stack([own_grad, got_grad]), jnp.stack([got_grad, own_grad]))
    return tokens_grad, full.T.astype(f32), up_grad, down_grad


def solution(mesh):
    fine = Mesh(mesh.devices.reshape(2, 2, Y, ZL, XH, 2), ("zh", "core", "y", "zl", "xh", "xl"))
    rows = P(EVERY_GROUP, ("zh", "core"), None)
    return jax.shard_map(
        on_device,
        mesh=fine,
        in_specs=(rows, P(), rows, rows, rows),
        out_specs=(rows, P(), rows, rows),
        check_vma=False,
    )
```

```python
import jax
import jax.numpy as jnp
import numpy as np
from jax import lax
from jax.experimental import pallas as pl
from jax.experimental.pallas import tpu as pltpu
from jax.sharding import Mesh, PartitionSpec as P

D = 1280
LANES = 128
WIDE = D + LANES
SLOTS = 64
Y, ZL, XH = 4, 8, 2
PLANE = ("y", "xh", "xl")
PLANE_CORES = ("core", "y", "xh", "xl")
COLUMN = ("zh", "zl")
ALL = ("zh", "core", "y", "zl", "xh", "xl")
EVERY_GROUP = ("y", "zl", "xh", "xl")
bf16, f32 = jnp.bfloat16, jnp.float32
NT = (((1,), (1,)), ((), ()))
TN = (((0,), (0,)), ((), ()))
SMEM = pl.BlockSpec(memory_space=pltpu.SMEM)
VMEM = pl.BlockSpec(memory_space=pltpu.VMEM)
ANY = pl.BlockSpec(memory_space=pl.ANY)
HBM = pl.BlockSpec(memory_space=pltpu.HBM)


def call(kernel, outs, *operands, after=(), stored=(), after_spec=None):
    first, last = len(operands), len(operands) + len(after)
    body = (lambda *refs: kernel(*refs[:first], *refs[last:])) if after else kernel
    bytes_accessed = sum(a.size * a.dtype.itemsize for a in (*operands, *outs, *stored))
    return pl.pallas_call(
        body,
        out_shape=[*outs, *stored],
        in_specs=[SMEM] + [VMEM] * (len(operands) - 1) + [after_spec or ANY] * len(after),
        out_specs=[VMEM] * len(outs) + [HBM] * len(stored),
        scratch_shapes=[pltpu.VMEM(a.shape, a.dtype) for a in stored] + [pltpu.SemaphoreType.DMA(())] * len(stored),
        compiler_params=pltpu.CompilerParams(vmem_limit_bytes=20 * 1024 * 1024),
        cost_estimate=pl.CostEstimate(flops=0, bytes_accessed=bytes_accessed, transcendentals=0),
    )(*operands, *after)


def shaped(shape, dtype):
    return jax.ShapeDtypeStruct(shape, dtype)


def pieces(value):
    first = value.astype(bf16).astype(f32)
    second = (value - first).astype(bf16).astype(f32)
    third = (value - first - second).astype(bf16).astype(f32)
    return [first, second, third]


def lanes_of(columns):
    rows = columns[0].shape[0]
    lane = lax.broadcasted_iota(jnp.int32, (rows, LANES), 1)
    packed = jnp.zeros((rows, LANES), f32)
    for k, column in enumerate(columns):
        packed = jnp.where(lane == k, column, packed)
    return packed


def three(stats, first):
    return stats[:, first : first + 1] + stats[:, first + 1 : first + 2] + stats[:, first + 2 : first + 3]


def combine_of(logits):
    raised = jnp.exp(logits - jnp.max(logits, axis=0, keepdims=True))
    return raised / jnp.sum(raised, axis=0, keepdims=True)


def slot_order(transpose=False):
    own = lax.broadcasted_iota(jnp.int32, (SLOTS, SLOTS), 1 if transpose else 0)
    expert = lax.broadcasted_iota(jnp.int32, (SLOTS, SLOTS), 0 if transpose else 1)
    return jnp.where(expert == ((own >> 1) & 3) * 16 + (own >> 3) * 2 + (own & 1), 1.0, 0.0).astype(bf16)


def merged(on_first, halves):
    tops = [three(h[:, D:], 0) for h in halves]
    totals = [three(h[:, D:], 3) for h in halves]
    top = jnp.maximum(tops[0], tops[1])
    parts = [totals[h] * jnp.exp(tops[h] - top) for h in range(2)]
    total = parts[0] + parts[1]
    shares = [jnp.where(on_first, part / total, 1.0) for part in parts]
    return halves[0][:, :D] * shares[0] + halves[1][:, :D] * shares[1], top, total


def slots_kernel(where_am_i, router_t, tok_own, tok_b, grad_own, grad_b, out):
    core = where_am_i[0]
    tok = jnp.concatenate([tok_own[...], tok_b[core]], axis=0)
    grad = jnp.concatenate([grad_own[...], grad_b[core]], axis=0)
    logits = lax.dot_general(router_t[...], tok, NT, preferred_element_type=f32)
    top = jnp.max(logits, axis=1, keepdims=True)
    raised = jnp.exp(logits - top)
    total = jnp.sum(raised, axis=1, keepdims=True)
    stats = lanes_of(pieces(top) + pieces(total))
    part_in = jnp.dot((raised / total).astype(bf16), tok, preferred_element_type=f32)
    part_grad = jnp.dot(combine_of(logits).astype(bf16), grad, preferred_element_type=f32)
    for zl in range(ZL):
        at = slice(zl * 8, zl * 8 + 8)
        for zh in range(2):
            place = zh * ZL + zl
            out[place, 0, :, :D] = part_in[at].astype(bf16)
            out[place, 1, :, :D] = part_grad[at].astype(bf16)
            out[place, 0, :, D:] = stats[at].astype(bf16)
            out[place, 1, :, D:] = stats[at].astype(bf16)


def middle(got, out, kept, stats_out):
    halves = [got[h * ZL : (h + 1) * ZL].astype(f32).reshape(LANES, WIDE) for h in range(2)]
    weighed = (lax.broadcasted_iota(jnp.int32, (LANES, 1), 0) & 8) == 0
    summed, top, total = merged(weighed, halves)
    kept[...] = summed
    stats_out[...] = lanes_of([top, total])
    row = lax.broadcasted_iota(jnp.int32, (LANES, LANES), 0)
    col = lax.broadcasted_iota(jnp.int32, (LANES, LANES), 1)
    source = (row & 7) * 16 + (row & 8) + (row >> 4)
    pick = jnp.where(col == source, 1.0, 0.0).astype(bf16)
    sorted_rows = jnp.dot(pick, summed.astype(bf16), preferred_element_type=f32)
    for yx in range(Y * XH):
        for array in range(2):
            at = yx * 16 + array * 8
            for xl in range(2):
                out[2 * yx + xl, array, :, :D] = sorted_rows[at : at + 8].astype(bf16)


def array_rows(ref, array):
    return ref[:, array, :, :D].astype(f32).reshape(LANES, D).astype(bf16)


def expert(rows, up_own, up_other, down_own, down_other, out, pre_grads, hiddens):
    slot_in, slot_grad = array_rows(rows, 0), array_rows(rows, 1)
    in_grad = jnp.zeros((LANES, D), f32)
    slot_out = jnp.zeros((LANES, D), f32)
    for j, (w_up, w_down) in enumerate(((up_own, down_own), (up_other, down_other))):
        pre_act = lax.dot_general(w_up[...], slot_in, NT, preferred_element_type=f32)
        hid_grad = lax.dot_general(w_down[...], slot_grad, NT, preferred_element_type=f32)
        cdf = 0.5 * (1.0 + lax.erf(pre_act * 0.7071067811865476))
        density = jnp.exp(pre_act * pre_act * -0.5) * 0.3989422804014327
        hiddens[j] = (pre_act * cdf).astype(bf16)
        pre_grads[j] = (hid_grad * (cdf + pre_act * density)).astype(bf16)
        in_grad += lax.dot_general(pre_grads[j], w_up[...], TN, preferred_element_type=f32)
        slot_out += lax.dot_general(hiddens[j], w_down[...], TN, preferred_element_type=f32)
    out[:, 0, :, :D] = in_grad.reshape(16, 8, D).astype(bf16)
    out[:, 1, :, :D] = slot_out.reshape(16, 8, D).astype(bf16)


def weight_grads(pre_grads, hiddens, rows, keep, send):
    slot_in, slot_grad = array_rows(rows, 0), array_rows(rows, 1)
    for j, out in enumerate((keep, send)):
        out[0] = jnp.dot(pre_grads[j], slot_in, preferred_element_type=f32).astype(bf16)
        out[1] = jnp.dot(hiddens[j], slot_grad, preferred_element_type=f32).astype(bf16)


def back_to_owners(got, kept, stats, out):
    row = lax.broadcasted_iota(jnp.int32, (LANES, 2 * LANES), 0)
    col = lax.broadcasted_iota(jnp.int32, (LANES, 2 * LANES), 1)
    source = (row & 7) * 32 + (row & 8) + (row >> 4)
    pick = jnp.where((col & ~16) == source, 1.0, 0.0).astype(bf16)
    rows = got[:, :, :, :D].astype(f32).reshape(2 * LANES, D).astype(bf16)
    summed = jnp.dot(pick, rows, preferred_element_type=f32).astype(bf16).astype(f32)
    share = jnp.sum(kept[...] * summed, axis=1, keepdims=True)
    top, total = stats[:, 0:1], stats[:, 1:2]
    extra = lanes_of(pieces(share) + pieces(top) + pieces(total))
    for zl in range(ZL):
        for array in range(2):
            at = slice(zl * 16 + array * 8, zl * 16 + array * 8 + 8)
            for zh in range(2):
                out[zh * ZL + zl, array, :, :D] = summed[at].astype(bf16)
                out[zh * ZL + zl, array, :, D:] = extra[at].astype(bf16)


def phase_2(where_am_i, got, slots, out, kept, stats):
    @pl.when(where_am_i[0] == 1)
    def _():
        middle(got, out, kept, stats)

    @pl.when(where_am_i[0] == 0)
    def _():
        out[...] = slots[...]


def phase_3(where_am_i, got, up_own, up_other, down_own, down_other, out, kept, stats, pre_grads, hiddens):
    @pl.when(where_am_i[0] == 1)
    def _():
        expert(got, up_own, up_other, down_own, down_other, out, pre_grads, hiddens)

    @pl.when(where_am_i[0] == 0)
    def _():
        middle(got, out, kept, stats)


def phase_4(where_am_i, got, kept, stats, up_own, up_other, down_own, down_other, out, pre_grads, hiddens):
    @pl.when(where_am_i[0] == 1)
    def _():
        back_to_owners(got, kept, stats, out)

    @pl.when(where_am_i[0] == 0)
    def _():
        expert(got, up_own, up_other, down_own, down_other, out, pre_grads, hiddens)


def phase_5(
    where_am_i, got, kept, stats, tok_a, tok_b, grad_a, grad_b, out, tok_store, grad_store, tok, grad, *done
):
    core = where_am_i[0]
    tok[:64], tok[64:] = tok_a[core], tok_b[core]
    grad[:64], grad[64:] = grad_a[core], grad_b[core]
    copies = [
        pltpu.make_async_copy(source, target, done[k])
        for k, (source, target) in enumerate(((tok, tok_store), (grad, grad_store)))
    ]
    for copy in copies:
        copy.start()

    @pl.when(core == 0)
    def _():
        back_to_owners(got, kept, stats, out)

    @pl.when(core == 1)
    def _():
        out[...] = got[...]

    for copy in copies:
        copy.wait()


def weights_kernel(where_am_i, pre_3, hid_3, rows_3, pre_4, hid_4, rows_4, keep, send):
    @pl.when(where_am_i[0] == 1)
    def _():
        weight_grads(pre_3, hid_3, rows_3, keep, send)

    @pl.when(where_am_i[0] == 0)
    def _():
        weight_grads(pre_4, hid_4, rows_4, keep, send)


def tokens_kernel(where_am_i, router_t, tok, grad, got_4, got_5, router_grad, left, right):
    spans = [slice(h * ZL, (h + 1) * ZL) for h in range(2)]
    halves = [jnp.where(where_am_i[0] == 1, got_4[span], got_5[span]).astype(f32) for span in spans]
    both = halves[0] + halves[1]
    slot_in_grad = both[:, 0, :, :D].reshape(SLOTS, D).astype(bf16)
    slot_out = both[:, 1, :, :D].reshape(SLOTS, D).astype(bf16)
    weighted = three(both[:, 0, :, D:].reshape(SLOTS, LANES), 0)
    stats = halves[0][:, 0, :, D:].reshape(SLOTS, LANES)
    top, total = three(stats, 3), three(stats, 6)
    logits = lax.dot_general(router_t[...], tok[...], NT, preferred_element_type=f32)
    dispatch = jnp.exp(logits - top) / total
    combine = combine_of(logits)
    cgrad = lax.dot_general(slot_out, grad[...], NT, preferred_element_type=f32)
    dgrad = lax.dot_general(slot_in_grad, tok[...], NT, preferred_element_type=f32)
    comb_part = combine * (cgrad - jnp.sum(combine * cgrad, axis=0, keepdims=True))
    disp_part = dispatch * (dgrad - weighted)
    logit_grad = (comb_part + disp_part).astype(bf16)
    by_expert = jnp.dot(slot_order(transpose=True), logit_grad, preferred_element_type=f32).astype(bf16)
    rows = jnp.dot(by_expert, tok[...], preferred_element_type=f32).astype(bf16)
    for k in range(SLOTS // 2):
        router_grad[k] = rows[2 * k : 2 * k + 2]
    left[:SLOTS], left[SLOTS:] = dispatch.astype(bf16), logit_grad
    right[...] = slot_in_grad


def tokens_grad_kernel(where_am_i, left, right, router_t, own_grad, sent_grad):
    both = jnp.concatenate([right[...], router_t[...]], axis=0)
    all_grad = lax.dot_general(left[...], both, TN, preferred_element_type=f32).astype(bf16)
    own_grad[...] = all_grad[:64]
    sent_grad[...] = all_grad[64:]


def spread_kernel(where_am_i, got, out):
    summed = jnp.sum(got[...].astype(f32), axis=0).astype(bf16)
    for k in range(out.shape[0]):
        out[k] = summed


def swap(value):
    return lax.ppermute(value, "core", [(0, 1), (1, 0)])


def exchange(value, axes):
    return lax.all_to_all(value, axes, split_axis=0, concat_axis=0, tiled=True)


def mixed(value, first_axes, second_axes):
    ids = np.arange(512).reshape(2, 2, Y, ZL, XH, 2)
    orders = {PLANE: (0, 2, 1, 3, 4), COLUMN: (1, 3, 4, 0, 2)}
    groups = [ids[:, core].transpose(orders[axes]).reshape(16, 16) for core, axes in enumerate((first_axes, second_axes))]
    return lax.all_to_all(
        value, ALL, split_axis=0, concat_axis=0, tiled=True, axis_index_groups=np.concatenate(groups).tolist()
    )


def on_device(tokens, router, up_proj, down_proj, out_grad):
    here = lax.axis_index("core").astype(jnp.int32).reshape(1)
    tok_b, grad_b = swap(tokens), swap(out_grad)
    on_first = here[0] == 0
    tok_own = jnp.where(on_first, tokens[0], tokens[1])
    grad_own = jnp.where(on_first, out_grad[0], out_grad[1])
    router_t = router.T.reshape(Y, ZL, XH, D).transpose(1, 0, 2, 3).reshape(SLOTS, D)
    wide = shaped((16, 2, 8, WIDE), bf16)
    acts = [shaped((2, 320, LANES), bf16)] * 2
    held = [shaped((LANES, D), f32), shaped((LANES, LANES), f32)]
    (slots,) = call(slots_kernel, [wide], here, router_t, tok_own, tok_b, grad_own, grad_b)
    got_1 = mixed(slots, PLANE, COLUMN)
    up_other, down_other = swap(up_proj[0]), swap(down_proj[0])
    weights = (up_proj[0], up_other, down_proj[0], down_other)
    sent_2, kept_1, stats_1 = call(phase_2, [wide, *held], here, got_1, slots, after=weights, after_spec=VMEM)
    got_2 = mixed(sent_2, COLUMN, PLANE)
    sent_3, kept_0, stats_0, pre_1, hid_1 = call(phase_3, [shaped((16, 2, 8, D), bf16), *held, *acts], here, got_2, *weights)
    got_3 = exchange(sent_3, PLANE)
    sent_4, pre_0, hid_0 = call(phase_4, [wide, *acts], here, got_3, kept_1, stats_1, *weights)
    got_4 = mixed(sent_4, PLANE, COLUMN)
    keep, send = call(
        weights_kernel, [shaped((2, 320, D), bf16), shaped((2, 320, D), bf16)],
        here, pre_1, hid_1, got_2, pre_0, hid_0, got_3,
    )
    got_send = swap(send)
    up_grad, down_grad = ((keep[k : k + 1].astype(f32) + got_send[k : k + 1].astype(f32)).astype(bf16) for k in range(2))
    sent_5, tok, grad = call(
        phase_5, [wide], here, got_4, kept_0, stats_0, tokens, tok_b, out_grad, grad_b,
        stored=[shaped((LANES, D), bf16)] * 2,
    )
    got_5 = mixed(sent_5, COLUMN, PLANE)
    router_part, left, right = call(
        tokens_kernel,
        [shaped((32, 2, D), bf16), shaped((LANES, LANES), bf16), shaped((SLOTS, D), bf16)],
        here, router_t, tok, grad, got_4, got_5, after=(up_grad, down_grad),
    )
    own_grad, sent_grad = call(
        tokens_grad_kernel, [shaped((64, D), bf16), shaped((64, D), bf16)], here, left, right, router_t
    )
    got_grad = swap(sent_grad)
    (part,) = call(
        spread_kernel, [shaped((16, 2, D), bf16)], here, exchange(router_part, PLANE_CORES)
    )
    (whole,) = call(spread_kernel, [shaped((32, 2, D), bf16)], here, exchange(part, COLUMN))
    full = exchange(whole, PLANE_CORES).reshape(SLOTS, D)
    tokens_grad = jnp.where(on_first, jnp.stack([own_grad, got_grad]), jnp.stack([got_grad, own_grad]))
    return tokens_grad, full.T.astype(f32), up_grad, down_grad


def solution(mesh):
    fine = Mesh(mesh.devices.reshape(2, 2, Y, ZL, XH, 2), ("zh", "core", "y", "zl", "xh", "xl"))
    rows = P(EVERY_GROUP, ("zh", "core"), None)
    return jax.shard_map(
        on_device,
        mesh=fine,
        in_specs=(rows, P(), rows, rows, rows),
        out_specs=(rows, P(), rows, rows),
        check_vma=False,
    )
```

```python
import jax
import jax.numpy as jnp
import numpy as np
from jax import lax
from jax.experimental import pallas as pl
from jax.experimental.pallas import tpu as pltpu
from jax.sharding import Mesh, PartitionSpec as P

D = 1280
LANES = 128
WIDE = D + LANES
SLOTS = 64
Y, ZL, XH = 4, 8, 2
PLANE = ("y", "xh", "xl")
PLANE_CORES = ("core", "y", "xh", "xl")
COLUMN = ("zh", "zl")
ALL = ("zh", "core", "y", "zl", "xh", "xl")
EVERY_GROUP = ("y", "zl", "xh", "xl")
bf16, f32 = jnp.bfloat16, jnp.float32
NT = (((1,), (1,)), ((), ()))
TN = (((0,), (0,)), ((), ()))
SMEM = pl.BlockSpec(memory_space=pltpu.SMEM)
VMEM = pl.BlockSpec(memory_space=pltpu.VMEM)
ANY = pl.BlockSpec(memory_space=pl.ANY)
HBM = pl.BlockSpec(memory_space=pltpu.HBM)


def call(kernel, outs, *operands, after=(), stored=(), after_spec=None):
    first, last = len(operands), len(operands) + len(after)
    body = (lambda *refs: kernel(*refs[:first], *refs[last:])) if after else kernel
    bytes_accessed = sum(a.size * a.dtype.itemsize for a in (*operands, *outs, *stored))
    return pl.pallas_call(
        body,
        out_shape=[*outs, *stored],
        in_specs=[SMEM] + [VMEM] * (len(operands) - 1) + [after_spec or ANY] * len(after),
        out_specs=[VMEM] * len(outs) + [HBM] * len(stored),
        scratch_shapes=[pltpu.VMEM(a.shape, a.dtype) for a in stored] + [pltpu.SemaphoreType.DMA(())] * len(stored),
        compiler_params=pltpu.CompilerParams(vmem_limit_bytes=20 * 1024 * 1024),
        cost_estimate=pl.CostEstimate(flops=0, bytes_accessed=bytes_accessed, transcendentals=0),
    )(*operands, *after)


def shaped(shape, dtype):
    return jax.ShapeDtypeStruct(shape, dtype)


def pieces(value):
    first = value.astype(bf16).astype(f32)
    second = (value - first).astype(bf16).astype(f32)
    third = (value - first - second).astype(bf16).astype(f32)
    return [first, second, third]


def lanes_of(columns):
    rows = columns[0].shape[0]
    lane = lax.broadcasted_iota(jnp.int32, (rows, LANES), 1)
    packed = jnp.zeros((rows, LANES), f32)
    for k, column in enumerate(columns):
        packed = jnp.where(lane == k, column, packed)
    return packed


def three(stats, first):
    return stats[:, first : first + 1] + stats[:, first + 1 : first + 2] + stats[:, first + 2 : first + 3]


def combine_of(logits):
    raised = jnp.exp(logits - jnp.max(logits, axis=0, keepdims=True))
    return raised / jnp.sum(raised, axis=0, keepdims=True)


def slot_order(transpose=False):
    own = lax.broadcasted_iota(jnp.int32, (SLOTS, SLOTS), 1 if transpose else 0)
    expert = lax.broadcasted_iota(jnp.int32, (SLOTS, SLOTS), 0 if transpose else 1)
    return jnp.where(expert == ((own >> 1) & 3) * 16 + (own >> 3) * 2 + (own & 1), 1.0, 0.0).astype(bf16)


def merged(on_first, halves):
    tops = [three(h[:, D:], 0) for h in halves]
    totals = [three(h[:, D:], 3) for h in halves]
    top = jnp.maximum(tops[0], tops[1])
    parts = [totals[h] * jnp.exp(tops[h] - top) for h in range(2)]
    total = parts[0] + parts[1]
    shares = [jnp.where(on_first, part / total, 1.0) for part in parts]
    return halves[0][:, :D] * shares[0] + halves[1][:, :D] * shares[1], top, total


def slots_kernel(where_am_i, router_t, tok_own, tok_b, grad_own, grad_b, out):
    core = where_am_i[0]
    tok = jnp.concatenate([tok_own[...], tok_b[core]], axis=0)
    grad = jnp.concatenate([grad_own[...], grad_b[core]], axis=0)
    logits = lax.dot_general(router_t[...], tok, NT, preferred_element_type=f32)
    top = jnp.max(logits, axis=1, keepdims=True)
    raised = jnp.exp(logits - top)
    total = jnp.sum(raised, axis=1, keepdims=True)
    stats = lanes_of(pieces(top) + pieces(total))
    part_in = jnp.dot((raised / total).astype(bf16), tok, preferred_element_type=f32)
    part_grad = jnp.dot(combine_of(logits).astype(bf16), grad, preferred_element_type=f32)
    for zl in range(ZL):
        at = slice(zl * 8, zl * 8 + 8)
        for zh in range(2):
            place = zh * ZL + zl
            out[place, 0, :, :D] = part_in[at].astype(bf16)
            out[place, 1, :, :D] = part_grad[at].astype(bf16)
            out[place, 0, :, D:] = stats[at].astype(bf16)
            out[place, 1, :, D:] = stats[at].astype(bf16)


def middle(got, out, kept, stats_out):
    halves = [got[h * ZL : (h + 1) * ZL].astype(f32).reshape(LANES, WIDE) for h in range(2)]
    weighed = (lax.broadcasted_iota(jnp.int32, (LANES, 1), 0) & 8) == 0
    summed, top, total = merged(weighed, halves)
    kept[...] = summed
    stats_out[...] = lanes_of([top, total])
    row = lax.broadcasted_iota(jnp.int32, (LANES, LANES), 0)
    col = lax.broadcasted_iota(jnp.int32, (LANES, LANES), 1)
    source = (row & 7) * 16 + (row & 8) + (row >> 4)
    pick = jnp.where(col == source, 1.0, 0.0).astype(bf16)
    sorted_rows = jnp.dot(pick, summed.astype(bf16), preferred_element_type=f32)
    for yx in range(Y * XH):
        for array in range(2):
            at = yx * 16 + array * 8
            for xl in range(2):
                out[2 * yx + xl, array, :, :D] = sorted_rows[at : at + 8].astype(bf16)


def array_rows(ref, array):
    return ref[:, array, :, :D].astype(f32).reshape(LANES, D).astype(bf16)


def expert(rows, up_own, up_other, down_own, down_other, out, pre_grads, hiddens):
    slot_in, slot_grad = array_rows(rows, 0), array_rows(rows, 1)
    in_grad = jnp.zeros((LANES, D), f32)
    slot_out = jnp.zeros((LANES, D), f32)
    for j, (w_up, w_down) in enumerate(((up_own, down_own), (up_other, down_other))):
        pre_act = lax.dot_general(w_up[...], slot_in, NT, preferred_element_type=f32)
        hid_grad = lax.dot_general(w_down[...], slot_grad, NT, preferred_element_type=f32)
        cdf = 0.5 * (1.0 + lax.erf(pre_act * 0.7071067811865476))
        density = jnp.exp(pre_act * pre_act * -0.5) * 0.3989422804014327
        hiddens[j] = (pre_act * cdf).astype(bf16)
        pre_grads[j] = (hid_grad * (cdf + pre_act * density)).astype(bf16)
        in_grad += lax.dot_general(pre_grads[j], w_up[...], TN, preferred_element_type=f32)
        slot_out += lax.dot_general(hiddens[j], w_down[...], TN, preferred_element_type=f32)
    out[:, 0, :, :D] = in_grad.reshape(16, 8, D).astype(bf16)
    out[:, 1, :, :D] = slot_out.reshape(16, 8, D).astype(bf16)


def weight_grads(pre_grads, hiddens, rows, keep, send):
    slot_in, slot_grad = array_rows(rows, 0), array_rows(rows, 1)
    for j, out in enumerate((keep, send)):
        out[0] = jnp.dot(pre_grads[j], slot_in, preferred_element_type=f32).astype(bf16)
        out[1] = jnp.dot(hiddens[j], slot_grad, preferred_element_type=f32).astype(bf16)


def back_to_owners(got, kept, stats, out):
    row = lax.broadcasted_iota(jnp.int32, (LANES, 2 * LANES), 0)
    col = lax.broadcasted_iota(jnp.int32, (LANES, 2 * LANES), 1)
    source = (row & 7) * 32 + (row & 8) + (row >> 4)
    pick = jnp.where((col & ~16) == source, 1.0, 0.0).astype(bf16)
    rows = got[:, :, :, :D].astype(f32).reshape(2 * LANES, D).astype(bf16)
    summed = jnp.dot(pick, rows, preferred_element_type=f32).astype(bf16).astype(f32)
    share = jnp.sum(kept[...] * summed, axis=1, keepdims=True)
    top, total = stats[:, 0:1], stats[:, 1:2]
    extra = lanes_of(pieces(share) + pieces(top) + pieces(total))
    for zl in range(ZL):
        for array in range(2):
            at = slice(zl * 16 + array * 8, zl * 16 + array * 8 + 8)
            for zh in range(2):
                out[zh * ZL + zl, array, :, :D] = summed[at].astype(bf16)
                out[zh * ZL + zl, array, :, D:] = extra[at].astype(bf16)


def phase_2(where_am_i, got, slots, out, kept, stats):
    @pl.when(where_am_i[0] == 0)
    def _():
        middle(got, out, kept, stats)

    @pl.when(where_am_i[0] == 1)
    def _():
        out[...] = slots[...]


def phase_3(where_am_i, got, up_own, up_other, down_own, down_other, out, kept, stats, pre_grads, hiddens):
    @pl.when(where_am_i[0] == 0)
    def _():
        expert(got, up_own, up_other, down_own, down_other, out, pre_grads, hiddens)

    @pl.when(where_am_i[0] == 1)
    def _():
        middle(got, out, kept, stats)


def phase_4(where_am_i, got, kept, stats, up_own, up_other, down_own, down_other, out, pre_grads, hiddens):
    @pl.when(where_am_i[0] == 0)
    def _():
        back_to_owners(got, kept, stats, out)

    @pl.when(where_am_i[0] == 1)
    def _():
        expert(got, up_own, up_other, down_own, down_other, out, pre_grads, hiddens)


def phase_5(
    where_am_i, got, kept, stats, tok_a, tok_b, grad_a, grad_b, out, tok_store, grad_store, tok, grad, *done
):
    core = where_am_i[0]
    tok[:64], tok[64:] = tok_a[core], tok_b[core]
    grad[:64], grad[64:] = grad_a[core], grad_b[core]
    copies = [
        pltpu.make_async_copy(source, target, done[k])
        for k, (source, target) in enumerate(((tok, tok_store), (grad, grad_store)))
    ]
    for copy in copies:
        copy.start()

    @pl.when(core == 1)
    def _():
        back_to_owners(got, kept, stats, out)

    @pl.when(core == 0)
    def _():
        out[...] = got[...]

    for copy in copies:
        copy.wait()


def weights_kernel(where_am_i, pre_3, hid_3, rows_3, pre_4, hid_4, rows_4, keep, send):
    @pl.when(where_am_i[0] == 0)
    def _():
        weight_grads(pre_3, hid_3, rows_3, keep, send)

    @pl.when(where_am_i[0] == 1)
    def _():
        weight_grads(pre_4, hid_4, rows_4, keep, send)


def tokens_kernel(where_am_i, router_t, tok, grad, got_4, got_5, router_grad, left, right):
    spans = [slice(h * ZL, (h + 1) * ZL) for h in range(2)]
    halves = [jnp.where(where_am_i[0] == 0, got_4[span], got_5[span]).astype(f32) for span in spans]
    both = halves[0] + halves[1]
    slot_in_grad = both[:, 0, :, :D].reshape(SLOTS, D).astype(bf16)
    slot_out = both[:, 1, :, :D].reshape(SLOTS, D).astype(bf16)
    weighted = three(both[:, 0, :, D:].reshape(SLOTS, LANES), 0)
    stats = halves[0][:, 0, :, D:].reshape(SLOTS, LANES)
    top, total = three(stats, 3), three(stats, 6)
    logits = lax.dot_general(router_t[...], tok[...], NT, preferred_element_type=f32)
    dispatch = jnp.exp(logits - top) / total
    combine = combine_of(logits)
    cgrad = lax.dot_general(slot_out, grad[...], NT, preferred_element_type=f32)
    dgrad = lax.dot_general(slot_in_grad, tok[...], NT, preferred_element_type=f32)
    comb_part = combine * (cgrad - jnp.sum(combine * cgrad, axis=0, keepdims=True))
    disp_part = dispatch * (dgrad - weighted)
    logit_grad = (comb_part + disp_part).astype(bf16)
    by_expert = jnp.dot(slot_order(transpose=True), logit_grad, preferred_element_type=f32).astype(bf16)
    rows = jnp.dot(by_expert, tok[...], preferred_element_type=f32).astype(bf16)
    for k in range(SLOTS // 2):
        router_grad[k] = rows[2 * k : 2 * k + 2]
    left[:SLOTS], left[SLOTS:] = dispatch.astype(bf16), logit_grad
    right[...] = slot_in_grad


def tokens_grad_kernel(where_am_i, left, right, router_t, own_grad, sent_grad):
    both = jnp.concatenate([right[...], router_t[...]], axis=0)
    all_grad = lax.dot_general(left[...], both, TN, preferred_element_type=f32).astype(bf16)
    own_grad[...] = all_grad[:64]
    sent_grad[...] = all_grad[64:]


def spread_kernel(where_am_i, got, out):
    summed = jnp.sum(got[...].astype(f32), axis=0).astype(bf16)
    for k in range(out.shape[0]):
        out[k] = summed


def swap(value):
    return lax.ppermute(value, "core", [(0, 1), (1, 0)])


def exchange(value, axes):
    return lax.all_to_all(value, axes, split_axis=0, concat_axis=0, tiled=True)


def mixed(value, first_axes, second_axes):
    ids = np.arange(512).reshape(2, 2, Y, ZL, XH, 2)
    orders = {PLANE: (0, 2, 1, 3, 4), COLUMN: (1, 3, 4, 0, 2)}
    groups = [ids[:, core].transpose(orders[axes]).reshape(16, 16) for core, axes in enumerate((first_axes, second_axes))]
    return lax.all_to_all(
        value, ALL, split_axis=0, concat_axis=0, tiled=True, axis_index_groups=np.concatenate(groups).tolist()
    )


def on_device(tokens, router, up_proj, down_proj, out_grad):
    here = lax.axis_index("core").astype(jnp.int32).reshape(1)
    tok_b, grad_b = swap(tokens), swap(out_grad)
    on_first = here[0] == 0
    tok_own = jnp.where(on_first, tokens[0], tokens[1])
    grad_own = jnp.where(on_first, out_grad[0], out_grad[1])
    router_t = router.T.reshape(Y, ZL, XH, D).transpose(1, 0, 2, 3).reshape(SLOTS, D)
    wide = shaped((16, 2, 8, WIDE), bf16)
    acts = [shaped((2, 320, LANES), bf16)] * 2
    held = [shaped((LANES, D), f32), shaped((LANES, LANES), f32)]
    (slots,) = call(slots_kernel, [wide], here, router_t, tok_own, tok_b, grad_own, grad_b)
    got_1 = mixed(slots, COLUMN, PLANE)
    up_other, down_other = swap(up_proj[0]), swap(down_proj[0])
    weights = (up_proj[0], up_other, down_proj[0], down_other)
    sent_2, kept_1, stats_1 = call(phase_2, [wide, *held], here, got_1, slots, after=weights, after_spec=VMEM)
    got_2 = mixed(sent_2, PLANE, COLUMN)
    sent_3, kept_0, stats_0, pre_1, hid_1 = call(phase_3, [shaped((16, 2, 8, D), bf16), *held, *acts], here, got_2, *weights)
    got_3 = exchange(sent_3, PLANE)
    sent_4, pre_0, hid_0 = call(phase_4, [wide, *acts], here, got_3, kept_1, stats_1, *weights)
    got_4 = mixed(sent_4, COLUMN, PLANE)
    keep, send = call(
        weights_kernel, [shaped((2, 320, D), bf16), shaped((2, 320, D), bf16)],
        here, pre_1, hid_1, got_2, pre_0, hid_0, got_3,
    )
    got_send = swap(send)
    up_grad, down_grad = ((keep[k : k + 1].astype(f32) + got_send[k : k + 1].astype(f32)).astype(bf16) for k in range(2))
    sent_5, tok, grad = call(
        phase_5, [wide], here, got_4, kept_0, stats_0, tokens, tok_b, out_grad, grad_b,
        stored=[shaped((LANES, D), bf16)] * 2,
    )
    got_5 = mixed(sent_5, PLANE, COLUMN)
    router_part, left, right = call(
        tokens_kernel,
        [shaped((32, 2, D), bf16), shaped((LANES, LANES), bf16), shaped((SLOTS, D), bf16)],
        here, router_t, tok, grad, got_4, got_5, after=(up_grad, down_grad),
    )
    own_grad, sent_grad = call(
        tokens_grad_kernel, [shaped((64, D), bf16), shaped((64, D), bf16)], here, left, right, router_t
    )
    got_grad = swap(sent_grad)
    (part,) = call(
        spread_kernel, [shaped((16, 2, D), bf16)], here, exchange(router_part, PLANE_CORES)
    )
    (whole,) = call(spread_kernel, [shaped((32, 2, D), bf16)], here, exchange(part, COLUMN))
    full = exchange(whole, PLANE_CORES).reshape(SLOTS, D)
    tokens_grad = jnp.where(on_first, jnp.stack([own_grad, got_grad]), jnp.stack([got_grad, own_grad]))
    return tokens_grad, full.T.astype(f32), up_grad, down_grad


def solution(mesh):
    fine = Mesh(mesh.devices.reshape(2, 2, Y, ZL, XH, 2), ("zh", "core", "y", "zl", "xh", "xl"))
    rows = P(EVERY_GROUP, ("zh", "core"), None)
    return jax.shard_map(
        on_device,
        mesh=fine,
        in_specs=(rows, P(), rows, rows, rows),
        out_specs=(rows, P(), rows, rows),
        check_vma=False,
    )
```
